128 devices in a mesh: expert: 4 (over z_lo, core), hidden: 32 (over x, z_hi, y).
Axes of the slice: x: 4, y: 4, z: 4 (z_hi: 2, z_lo: 2; z = z_hi * 2 + z_lo), core: 2. Of those that a mesh axis runs over, the one named last changes fastest.
Arguments:
- tokens: bfloat16 [1536, 6144], P(('expert', 'hidden')), may hold values from -6 to 6
- routes: int32 [1536, 2], P(('expert', 'hidden')), may hold values from 0 to 3, all different within a row; in each aligned block of 12 rows (0 to 11, 12 to 23, ...) at most 8 rows name the same one
- combine: float32 [1536, 2], P(('expert', 'hidden')), may hold values from 0.25 to 1
- gate_weight: bfloat16 [4, 6144, 16384], P('expert', None, 'hidden'), may hold values from -0.078125 to 0.078125
- up_weight: bfloat16 [4, 6144, 16384], P('expert', None, 'hidden'), may hold values from -0.078125 to 0.078125
- down_weight: bfloat16 [4, 16384, 6144], P('expert', 'hidden'), may hold values from -0.046875 to 0.046875
Outputs:
- mixed: bfloat16 [1536, 6144], P(('expert', 'hidden'))
The draws below stay inside these ranges and needn't reach their ends.
Inputs may be any that keep to these rules, and one draw needn't show every extreme that they name: `routes`: within each aligned block of 12 tokens, the 2 experts of a token differ and no expert is chosen by more than 8 tokens; in some blocks one expert is chosen by exactly 8 tokens.
All inputs are finite; a program needn't handle non-finite values.
Results may differ from the reference program's by a relative error of at most 0.0049.
Values may be sent and summed in bfloat16 or wider, within the bound.
A program may use at most 192 MiB of HBM per device.

```python
import math
import jax
import jax.numpy as jnp
import numpy as np

D = 6144
FF = 16384
TOP = 2
TOK_DEV = 12
EXPERTS = 4
CAP = 8
TOKENS = 1536
N_EXPERT = 4
N_HIDDEN = 32


def shard_levels(own_key, shape, pieces, low, high):
    factor_of = 1.0
    for axis_at, shards_of in pieces:
        draws = jax.random.uniform(jax.random.fold_in(jax.random.fold_in(own_key, 6), axis_at), (shards_of,), jnp.float32, low / len(pieces), high / len(pieces))
        factor_of = factor_of * jnp.repeat(jnp.exp(draws), shape[axis_at] // shards_of).reshape((-1,) + (1,) * (len(shape) - 1 - axis_at))
    return factor_of


def shared_out(key, own, number, rows, amount, top, limit, skew):
    ranking = jax.random.permutation(key, amount)
    packed, usual = load_shares(amount, rows * top, limit, skew, True), load_shares(amount, rows * top, limit, skew, False)
    places = jnp.arange(amount)

    def named(tallies, rotation):
        used = int((tallies > 0).sum())
        fixed = max(1, used // 4)
        passed = fixed + (places - fixed + rotation * (used - fixed)) % max(1, amount - fixed)
        return jnp.zeros((amount,), jnp.int32).at[ranking[jnp.where(places < fixed, places, passed)]].set(jnp.asarray(tallies, jnp.int32))

    tallies = jnp.where(number % 4 == 0, named(packed, number // 4), named(usual, number - number // 4 - 1))
    mixed = jax.random.permutation(jax.random.fold_in(own, 3), amount)
    giver, sink = mixed[0:amount // 2 * 2:2], mixed[1:amount // 2 * 2:2]
    margin = jnp.minimum(tallies[giver] - 1, limit - tallies[sink]) // 2
    margin = jnp.where((giver == ranking[0]) | (sink == ranking[0]) | (tallies[sink] == 0), 0, jnp.maximum(margin, 0))
    passed = jax.random.randint(jax.random.fold_in(own, 4), (amount // 2,), 0, 1 << 20) % (margin + 1)
    tallies = tallies.at[giver].add(-passed).at[sink].add(passed)
    labels = jnp.searchsorted(jnp.cumsum(tallies), jnp.arange(rows * top), side="right").astype(jnp.int32)
    listing = labels.reshape(top, rows).T
    listing = listing[jax.random.permutation(jax.random.fold_in(own, 1), rows)]
    rotation = jax.random.randint(jax.random.fold_in(own, 2), (rows, 1), 0, top)
    return jnp.take_along_axis(listing, (jnp.arange(top)[None, :] + rotation) % top, axis=1)


def load_shares(amount, total, most, slope, full):
    weights = [(1 << 20) // math.isqrt(grade ** slope) + 1 for grade in range(1, amount + 1)]
    largest = most if full else min(most, max(-(-total // amount), total * weights[0] // sum(weights)))
    least = 1 if total - largest >= amount - 1 else 0
    holding, spare = [largest] + [least] * (amount - 1), total - largest - least * (amount - 1)
    while spare > 0:
        candidates = [i for i in range(1, amount) if holding[i] < largest] or [i for i in range(1, amount) if holding[i] < most]
        mass, remaining = sum([weights[i] for i in candidates]), spare
        for i in candidates:
            addition = min(most - holding[i], max(1, remaining * weights[i] // mass), spare)
            holding[i] = holding[i] + addition
            spare = spare - addition
    return np.array(holding)


def scatter_about(rng, shape, width, bound, split=(), kind=jnp.bfloat16):
    gain = shard_levels(rng, shape, split, -0.22, 0.18) if split else 1.0
    result = jax.random.normal(rng, shape, jnp.float32) * width * gain
    return jnp.minimum(jnp.maximum(result, -bound), bound).astype(kind)


def setup_inputs(seed: int = 0) -> dict:
    streams_of = jax.random.split(jax.random.key(seed), 7)
    tokens = scatter_about(streams_of[0], (TOKENS, D), 1.0, 6.0, ((0, 128),))
    routes_keys = jax.random.split(jax.random.fold_in(streams_of[1], 1), TOKENS // TOK_DEV)
    routes_turns = jax.random.permutation(jax.random.fold_in(streams_of[1], 3), TOKENS // TOK_DEV)
    routes = jax.vmap(lambda own, number: shared_out(jax.random.fold_in(streams_of[1], 2), own, number, TOK_DEV, EXPERTS, TOP, CAP, 2))(routes_keys, routes_turns).reshape((TOKENS, TOP))
    combine = jnp.clip(0.25 + 0.75 * jax.random.uniform(streams_of[2], (TOKENS, TOP), jnp.float32) ** shard_levels(streams_of[2], (TOKENS, TOP), ((0, 128),), -0.2, 0.2), 0.25, 1.0)
    gate_weight = scatter_about(streams_of[3], (EXPERTS, D, FF), D ** -0.5, 0.078125, ((0, 4), (2, 32)))
    up_weight = scatter_about(streams_of[4], (EXPERTS, D, FF), D ** -0.5, 0.078125, ((0, 4), (2, 32)))
    down_weight = scatter_about(streams_of[5], (EXPERTS, FF, D), FF ** -0.5, 0.046875, ((0, 4), (1, 32)))
    return {"tokens": tokens, "routes": routes, "combine": combine, "gate_weight": gate_weight, "up_weight": up_weight, "down_weight": down_weight}


def slot_indices(routes):
    blocks = routes.reshape(-1, TOK_DEV * TOP)
    chosen = (blocks[:, :, None] == jnp.arange(EXPERTS, dtype=jnp.int32)[None, None, :]).astype(jnp.int32)
    before = jnp.cumsum(chosen, axis=1) - chosen
    return jnp.sum(before * chosen, axis=2).reshape(-1, TOP).astype(jnp.int32)


def reference(tokens, routes, combine, gate_weight, up_weight, down_weight):
    slots = slot_indices(routes)
    total_rows = N_EXPERT * N_HIDDEN * CAP
    owner = (jnp.arange(TOKENS, dtype=jnp.int32) // TOK_DEV)[:, None]
    rows = (owner * CAP + slots).astype(jnp.int32)
    copies = jnp.repeat(tokens, TOP, axis=0)
    outputs = []
    for expert in range(EXPERTS):
        target = jnp.where(routes == expert, rows, total_rows).reshape(-1).astype(jnp.int32)
        buffer = jnp.zeros((total_rows, D), jnp.bfloat16).at[target].set(copies, mode="drop")
        gate_out = jnp.dot(buffer, gate_weight[expert], preferred_element_type=jnp.float32)
        up_out = jnp.dot(buffer, up_weight[expert], preferred_element_type=jnp.float32)
        hidden = (jax.nn.silu(gate_out) * up_out).astype(jnp.bfloat16)
        outputs.append(jnp.dot(hidden, down_weight[expert], preferred_element_type=jnp.float32))
    stacked = jnp.stack(outputs).reshape(EXPERTS * total_rows, D)
    index = (routes * total_rows + rows).astype(jnp.int32)
    picked = stacked[index]
    mixed = jnp.sum(combine[:, :, None] * picked, axis=1)
    return mixed.astype(jnp.bfloat16)
```

```python
import jax
import jax.numpy as jnp
from jax import lax
from jax.experimental import pallas as pl
from jax.experimental.pallas import tpu as pltpu
from jax.sharding import PartitionSpec as P

MESH = pl.DeviceIdType.MESH
BF16, F32 = jnp.bfloat16, jnp.float32
ROWS = 12
UNIT = 2 * ROWS
PAD = 32
GROUP = 4 * UNIT


def hot(axis):
    if isinstance(axis, int):
        return tuple(int(axis == j) for j in range(3))
    return (lax.div((2 - axis) * (1 - axis), 2), axis * (2 - axis), lax.div(axis * (axis - 1), 2))


class Place:
    def __init__(self):
        e, h = lax.axis_index("expert"), lax.axis_index("hidden")
        self.expert = e
        self.core = lax.rem(e, 2)
        self.at = (
            lax.div(h, 8),
            lax.rem(h, 4),
            lax.rem(lax.div(h, 4), 2) * 2 + lax.div(e, 2),
        )

    def device(self, at, core):
        x, y, z = at
        return {
            "expert": lax.rem(z, 2) * 2 + core,
            "hidden": x * 8 + lax.div(z, 2) * 4 + y,
        }

    def sibling(self):
        return self.device(self.at, 1 - self.core)

    def axis(self, p, k):
        return (p + k) % 3 if isinstance(p, int) else lax.rem(p + k, 3)

    def coord(self, p, k):
        return sum(a * o for a, o in zip(self.at, hot(self.axis(p, k))))

    def along(self, p, k, step):
        on = hot(self.axis(p, k))
        return self.device(tuple(lax.rem(a + step * o, 4) for a, o in zip(self.at, on)), self.core)

    def unit(self, p, i1, i2, i3):
        total = 0
        for k, i in enumerate((i1, i2, i3)):
            o = hot(self.axis(p, k))
            total = total + i * (16 * o[0] + 4 * o[1] + o[2])
        return total


def meet(place):
    barrier = pltpu.get_barrier_semaphore()
    partners = [place.sibling()]
    for a in range(3):
        partners += [place.along(a, 0, 1), place.along(a, 0, 3)]
    for partner in partners:
        pl.semaphore_signal(barrier, inc=1, device_id=partner, device_id_type=MESH)
    pl.semaphore_wait(barrier, len(partners))


def wires(send_sem, recv_sem):
    def wire(slot, src, dst, device):
        return pltpu.make_async_remote_copy(
            src_ref=src,
            dst_ref=dst,
            send_sem=send_sem.at[slot],
            recv_sem=recv_sem.at[slot],
            device_id=device,
            device_id_type=MESH,
        )

    return wire


def each(body):
    pl.loop(0, 3)(body)


def plus(i, n):
    return lax.rem(i + n, 4)


class Gather:
    def __init__(self, place, wire, base, k, pick, parts=1):
        self.place, self.wire, self.base, self.k, self.pick, self.parts = (
            place, wire, base, k, pick, parts,
        )

    slots = 12

    def own(self, p, half, step):
        ref = self.pick(p, half, self.place.coord(p, self.k))
        slot = self.base + (half * 2 + (0 if step == 1 else 1)) * 3 + p
        return self.wire(slot, ref, ref, self.place.along(p, self.k, step))

    def passed(self, p, half, part=0):
        i = plus(self.place.coord(p, self.k), 3 if half == 0 else 1)
        ref = self.pick(p, half, i)
        if self.parts > 1:
            n = ref.shape[0] // self.parts
            ref = ref.at[pl.ds(part * n, n)]
        slot = self.base + 12 + (part * 2 + half) * 3 + p
        return self.wire(slot, ref, ref, self.place.along(p, self.k, 1 if half == 0 else 3))

    def start(self, p):
        self.own(p, 0, 1).start()
        self.own(p, 1, 3).start()
        self.own(p, 1, 1).start()
        self.own(p, 0, 3).start()

    def middle(self, p):
        self.own(p, 0, 1).wait_recv()
        for n in range(self.parts):
            self.passed(p, 0, n).start()
        self.own(p, 1, 3).wait_recv()
        for n in range(self.parts):
            self.passed(p, 1, n).start()

    def near(self, p):
        self.own(p, 1, 1).wait_recv()
        self.own(p, 0, 3).wait_recv()

    def far(self, p):
        for n in range(self.parts):
            self.passed(p, 0, n).wait_recv()
            self.passed(p, 1, n).wait_recv()

    def sent(self, p):
        for half in range(2):
            self.own(p, half, 1).wait_send()
            self.own(p, half, 3).wait_send()
            for n in range(self.parts):
                self.passed(p, half, n).wait_send()


LAST = 4


def gather_kernel(
    t_ref, c_ref, gate_ref, up_ref, out_ref,
    w_ref, other, other_c, first, first_c, x_ref, table, acc, load_sem, send_sem, recv_sem,
):
    place = Place()
    core, sibling = place.core, place.sibling()
    wire = wires(send_sem, recv_sem)
    width = x_ref.shape[-1]
    ff = gate_ref.shape[1]
    part = 4 * width

    loads = [
        pltpu.make_async_copy(gate_ref, w_ref.at[:, pl.ds(0, ff)], load_sem.at[0]),
        pltpu.make_async_copy(up_ref, w_ref.at[:, pl.ds(ff, ff)], load_sem.at[1]),
    ]
    for load in loads:
        load.start()
    meet(place)

    trade = [
        wire(0, t_ref.at[1 - core], other, sibling),
        wire(1, c_ref, other_c, sibling),
    ]
    for t in trade:
        t.start()

    @pl.loop(0, acc.shape[0])
    def _(u):
        acc[u] = jnp.zeros(acc.shape[1:], F32)

    g1 = Gather(place, wire, 2, 0, lambda p, half, i: first.at[p, half, i])
    g2 = Gather(
        place, wire, 20, 1,
        lambda p, half, i: x_ref.at[p, 2 * core + half, place.coord(p, 2), i],
    )
    g3 = Gather(place, wire, 38, 2, lambda p, half, i: x_ref.at[p, 2 * core + half, i], LAST)
    table_base = 38 + 12 + 6 * LAST
    views = (
        lambda i: first_c.at[i],
        lambda i: table.at[place.coord(0, 2), i],
        lambda i: table.at[i],
    )

    def table_wire(k, n):
        me = place.coord(0, k)
        ref = views[k](me if n < 2 else plus(me, 3))
        return wire(table_base + 3 * k + n, ref, ref, place.along(0, k, 3 if n == 1 else 1))

    joined_base = table_base + 9

    def joined(p, i, kind, half=None, part=None):
        if half is None:
            ref = x_ref.at[p, pl.ds(2 * core, 2), i]
        elif part is None:
            ref = x_ref.at[p, 2 * core + half, i]
        else:
            n = 4 // LAST
            ref = x_ref.at[p, 2 * core + half, i, pl.ds(part * n, n)]
        return wire(joined_base + kind * 3 + p, ref, ref, sibling)

    for t in trade:
        t.wait_recv()

    @each
    def _(p):
        for half in range(2):
            first[p, half, place.coord(p, 0)] = t_ref[core, p, half] + other[p, half]
        g1.start(p)

    first_c[place.coord(0, 0)] = c_ref[...] + other_c[...]
    table_wire(0, 0).start()
    table_wire(0, 1).start()
    each(g1.middle)
    table_wire(0, 0).wait_recv()
    table_wire(0, 2).start()

    @each
    def _(p):
        g1.near(p)
        g1.far(p)
        for half in range(2):
            rows = jnp.concatenate(
                [first[p, half, i].astype(F32)[:UNIT] for i in range(4)], axis=0
            )
            x_ref[p, 2 * core + half, place.coord(p, 2), place.coord(p, 1)] = rows.astype(BF16)
        g2.start(p)

    table_wire(0, 1).wait_recv()
    table_wire(0, 2).wait_recv()
    table[place.coord(0, 2), place.coord(0, 1)] = (
        first_c[0] + first_c[1] + first_c[2] + first_c[3]
    )
    table_wire(1, 0).start()
    table_wire(1, 1).start()
    each(g2.middle)
    table_wire(1, 0).wait_recv()
    table_wire(1, 2).start()

    @each
    def _(p):
        g2.near(p)
        g2.far(p)
        g3.start(p)
        joined(p, place.coord(p, 2), 0).start()

    table_wire(1, 1).wait_recv()
    table_wire(1, 2).wait_recv()
    table_wire(2, 0).start()
    table_wire(2, 1).start()

    def gate_up(p, i3):
        @pl.loop(0, w_ref.shape[1] // ff)
        def _(n):
            cols = pl.ds(pl.multiple_of(n * ff, ff), ff)
            rows = jnp.concatenate(
                [x_ref[p, k, i3].reshape(4 * GROUP, width) for k in range(4)], axis=1
            )
            part_rows = pl.ds(pl.multiple_of(p * part, part), part)
            result = jnp.dot(rows, w_ref[part_rows, cols], preferred_element_type=F32)
            for i2 in range(4):
                for i1 in range(4):
                    at = (i2 * 4 + i1) * UNIT
                    u = place.unit(p, i1, i2, i3)
                    acc[u, :, cols] = acc[u, :, cols] + result[at : at + UNIT]

    for load in loads:
        load.wait()

    @each
    def _(p):
        joined(p, place.coord(p, 2), 0).wait_recv()
        gate_up(p, place.coord(p, 2))

    @each
    def _(p):
        me = place.coord(p, 2)
        g3.middle(p)
        joined(p, plus(me, 3), 1, 0).start()
        joined(p, plus(me, 1), 2, 1).start()

    table_wire(2, 0).wait_recv()
    table_wire(2, 2).start()

    @each
    def _(p):
        me = place.coord(p, 2)
        g3.near(p)
        joined(p, plus(me, 3), 3, 1).start()
        joined(p, plus(me, 1), 4, 0).start()

    @each
    def _(p):
        me = place.coord(p, 2)
        joined(p, plus(me, 3), 1, 0).wait_recv()
        joined(p, plus(me, 3), 3, 1).wait_recv()
        gate_up(p, plus(me, 3))

    @each
    def _(p):
        me = place.coord(p, 2)
        joined(p, plus(me, 1), 2, 1).wait_recv()
        joined(p, plus(me, 1), 4, 0).wait_recv()
        gate_up(p, plus(me, 1))

    for n in range(LAST):
        @each
        def _(p):
            me = place.coord(p, 2)
            for half in range(2):
                g3.passed(p, half, n).wait_recv()
                joined(p, plus(me, 2), 5 + 2 * n + half, half, n).start()

    @each
    def _(p):
        me = place.coord(p, 2)
        for n in range(LAST):
            for half in range(2):
                joined(p, plus(me, 2), 5 + 2 * n + half, half, n).wait_recv()
        gate_up(p, plus(me, 2))

    table_wire(2, 1).wait_recv()
    table_wire(2, 2).wait_recv()

    lane = lax.broadcasted_iota(jnp.int32, (UNIT, 128), 1)
    row = lax.broadcasted_iota(jnp.int32, (UNIT, 128), 0)
    token = jnp.where(row < ROWS, row, row - ROWS)
    chosen = lane == token * 4 + place.expert

    @pl.loop(0, 16)
    def _(yz):
        y, z = lax.div(yz, 4), lax.rem(yz, 4)
        own = table[z, y]
        for x in range(4):
            u = x * 16 + yz
            pair = jnp.where(row < ROWS, own[2 * x : 2 * x + 1], own[2 * x + 1 : 2 * x + 2])
            weight = jnp.sum(jnp.where(chosen, pair, 0.0), axis=1, keepdims=True)
            gate, up = acc[u, :, :ff], acc[u, :, ff:]
            out_ref[u, :, :ff] = gate / (1.0 + jnp.exp(-gate)) * up
            out_ref[u, :, ff:] = jnp.broadcast_to(weight, (UNIT, 128))

    for t in trade:
        t.wait_send()
    for k in range(3):
        for n in range(3):
            table_wire(k, n).wait_send()

    @each
    def _(p):
        me = place.coord(p, 2)
        for g in (g1, g2, g3):
            g.sent(p)
        joined(p, me, 0).wait_send()
        joined(p, plus(me, 3), 1, 0).wait_send()
        joined(p, plus(me, 1), 2, 1).wait_send()
        joined(p, plus(me, 3), 3, 1).wait_send()
        joined(p, plus(me, 1), 4, 0).wait_send()
        for n in range(LAST):
            for half in range(2):
                joined(p, plus(me, 2), 5 + 2 * n + half, half, n).wait_send()


GATHER_SLOTS = 38 + 12 + 6 * LAST + 9 + 3 * (5 + 2 * LAST)


class Reduce:
    slots = 18

    def __init__(self, place, wire, base, k, pick, far, plain, merged):
        self.place, self.wire, self.base, self.k, self.pick = place, wire, base, k, pick
        self.far, self.plain, self.merged = far, plain, merged

    def copy(self, p, n, d, half, into, step):
        return self.wire(
            self.base + n * 3 + p, self.pick(p, d, half), into.at[p, half],
            self.place.along(p, self.k, step),
        )

    def opposite(self, p, half):
        return self.copy(p, half, 2, half, self.far, 1 if half == 0 else 3)

    def direct(self, p, half):
        return self.copy(p, 2 + half, 1 if half == 1 else 3, half, self.plain, 1 if half == 1 else 3)

    def relayed(self, p, half):
        return self.copy(p, 4 + half, 1 if half == 0 else 3, half, self.merged, 1 if half == 0 else 3)

    def merge(self, p):
        for half in range(2):
            self.opposite(p, half).wait_recv()
            ref = self.pick(p, 1 if half == 0 else 3, half)
            ref[...] = (ref[...].astype(F32) + self.far[p, half].astype(F32)).astype(BF16)
            self.relayed(p, half).start()

    def total(self, p, half):
        self.direct(p, half).wait_recv()
        self.relayed(p, half).wait_recv()
        return (
            self.pick(p, 0, half)[...].astype(F32)
            + self.plain[p, half].astype(F32)
            + self.merged[p, half].astype(F32)
        )

    def sent(self, p):
        for half in range(2):
            self.opposite(p, half).wait_send()
            self.direct(p, half).wait_send()
            self.relayed(p, half).wait_send()


def reduce_kernel(
    h_ref, down_ref, out_ref,
    w_ref, hp, wp, give, take, own, far1, plain1, merged1,
    z2, far2, plain2, merged2, z3, far3, plain3, merged3, load_sem, send_sem, recv_sem,
):
    place = Place()
    core, sibling = place.core, place.sibling()
    wire = wires(send_sem, recv_sem)
    width = own.shape[-1]
    ff = down_ref.shape[0]

    def load(p, which):
        begin = p * 4 * width + (core if which == 0 else 1 - core) * 2 * width
        return pltpu.make_async_copy(
            down_ref.at[:, pl.ds(pl.multiple_of(begin, 2 * width), 2 * width)],
            w_ref.at[which, p],
            load_sem.at[which * 3 + p],
        )

    for which in (1, 0):
        for p in range(3):
            load(p, which).start()
    meet(place)

    r1 = Reduce(place, wire, 0, 2, lambda p, d, half: own.at[p, d, half], far1, plain1, merged1)
    r2 = Reduce(
        place, wire, 18, 1,
        lambda p, d, half: z2.at[p, half, plus(place.coord(p, 1), d)], far2, plain2, merged2,
    )
    r3 = Reduce(
        place, wire, 36, 0,
        lambda p, d, half: z3.at[p, half, plus(place.coord(p, 0), d)], far3, plain3, merged3,
    )

    def handed(p, d):
        return wire(54 + d * 3 + p, give.at[p, d], take.at[p, d], sibling)

    def product(p, which, half):
        cols = pl.ds(pl.multiple_of(half * width, width), width)
        scale = wp[p]
        return jnp.dot(
            hp[p], w_ref[which, p, :, cols], preferred_element_type=F32
        ) * jnp.concatenate([scale] * (width // 128), axis=1)

    def for_sibling(d):
        @each
        def _(p):
            i3 = plus(place.coord(p, 2), d)
            units = [place.unit(p, i1, i2, i3) for i2 in range(4) for i1 in range(4)]
            for i in range(4):
                rows = [h_ref[u] for u in units[4 * i : 4 * i + 4]]
                at = pl.ds(i * GROUP, GROUP)
                hp[p, at, :] = jnp.concatenate([r[:, :ff] for r in rows], axis=0).astype(BF16)
                wp[p, at, :] = jnp.concatenate([r[:, ff:] for r in rows], axis=0)

            @pl.loop(0, 2)
            def _(half):
                give[p, d, half] = product(p, 1, half).astype(BF16)

            handed(p, d).start()

    def for_chip(d):
        @each
        def _(p):
            handed(p, d).wait_recv()

            @pl.loop(0, 2)
            def _(half):
                total = product(p, 0, half) + take[p, d, half].astype(F32)
                own[p, d, half] = total.astype(BF16)

            if d == 2:
                r1.opposite(p, 0).start()
                r1.opposite(p, 1).start()
            elif d == 1:
                r1.direct(p, 1).start()
            elif d == 3:
                r1.direct(p, 0).start()

    for p in range(3):
        load(p, 1).wait()
    for_sibling(2)
    for p in range(3):
        load(p, 0).wait()
    for_chip(2)
    for d in (1, 3):
        for_sibling(d)
        for_chip(d)
    each(r1.merge)
    for_sibling(0)
    for_chip(0)

    @each
    def _(p):
        for half in range(2):
            total = r1.total(p, half)
            for i in range(4):
                z2[p, half, i] = total[i * GROUP : (i + 1) * GROUP].astype(BF16)
        r2.opposite(p, 0).start()
        r2.opposite(p, 1).start()
        r2.direct(p, 1).start()
        r2.direct(p, 0).start()

    each(r2.merge)

    @each
    def _(p):
        for half in range(2):
            total = r2.total(p, half)
            for i in range(4):
                rows = total[i * UNIT : (i + 1) * UNIT]
                rows = jnp.concatenate([rows, jnp.zeros((PAD - UNIT, width), F32)], axis=0)
                z3[p, half, i] = rows.astype(BF16)
        r3.opposite(p, 0).start()
        r3.opposite(p, 1).start()
        r3.direct(p, 1).start()
        r3.direct(p, 0).start()

    each(r3.merge)

    @each
    def _(p):
        for half in range(2):
            out_ref[core, p, half] = r3.total(p, half).astype(BF16)

    last = wire(66, out_ref.at[core], out_ref.at[core], sibling)
    last.start()

    @each
    def _(p):
        for r in (r1, r2, r3):
            r.sent(p)
        for d in range(4):
            handed(p, d).wait_send()

    last.wait_recv()
    last.wait_send()


REDUCE_SLOTS = 67


def on_device(tokens, routes, combine, gate_weight, up_weight, down_weight):
    width = tokens.shape[1] // 12
    ff = gate_weight.shape[2]
    place = Place()
    core = place.core
    slabs = tokens.reshape(ROWS, 3, 2, 2, width).transpose(2, 1, 3, 0, 4)
    slabs = lax.dynamic_update_slice(
        jnp.zeros((2, 3, 2, PAD, width), BF16), slabs, (0, 0, 0, ROWS * core, 0)
    )
    experts = jnp.arange(4, dtype=jnp.int32)
    dense = jnp.sum(
        jnp.where(routes[:, :, None] == experts, combine[:, :, None], 0.0), axis=1
    ).reshape(1, 4 * ROWS)
    dense = jnp.pad(dense, ((0, 0), (0, 128 - 4 * ROWS)))
    mine = jnp.arange(8, dtype=jnp.int32)[:, None] == 2 * place.at[0] + core
    dense = jnp.where(mine, dense, 0.0)

    vmem = pl.BlockSpec(memory_space=pltpu.VMEM)
    hbm = pl.BlockSpec(memory_space=pl.ANY)
    hidden = pl.pallas_call(
        gather_kernel,
        out_shape=jax.ShapeDtypeStruct((64, UNIT, ff + 128), F32),
        in_specs=[vmem, vmem, hbm, hbm],
        out_specs=vmem,
        scratch_shapes=[
            pltpu.VMEM((12 * width, 2 * ff), BF16),
            pltpu.VMEM((3, 2, PAD, width), BF16),
            pltpu.VMEM((8, 128), F32),
            pltpu.VMEM((3, 2, 4, PAD, width), BF16),
            pltpu.VMEM((4, 8, 128), F32),
            pltpu.VMEM((3, 4, 4, 4, GROUP, width), BF16),
            pltpu.VMEM((4, 4, 8, 128), F32),
            pltpu.VMEM((64, UNIT, 2 * ff), F32),
            pltpu.SemaphoreType.DMA((2,)),
            pltpu.SemaphoreType.DMA((GATHER_SLOTS,)),
            pltpu.SemaphoreType.DMA((GATHER_SLOTS,)),
        ],
        compiler_params=pltpu.CompilerParams(
            collective_id=0, has_side_effects=True, vmem_limit_bytes=60 * 2**20
        ),
    )(slabs, dense, gate_weight[0], up_weight[0])

    def three(*shape):
        return [pltpu.VMEM((3, 2) + shape + (width,), BF16) for _ in range(3)]

    out = pl.pallas_call(
        reduce_kernel,
        out_shape=jax.ShapeDtypeStruct((2, 3, 2, PAD, width), BF16),
        in_specs=[vmem, hbm],
        out_specs=vmem,
        scratch_shapes=[
            pltpu.VMEM((2, 3, ff, 2 * width), BF16),
            pltpu.VMEM((3, 4 * GROUP, ff), BF16),
            pltpu.VMEM((3, 4 * GROUP, 128), F32),
            pltpu.VMEM((3, 4, 2, 4 * GROUP, width), BF16),
            pltpu.VMEM((3, 4, 2, 4 * GROUP, width), BF16),
            pltpu.VMEM((3, 4, 2, 4 * GROUP, width), BF16),
            *three(4 * GROUP),
            pltpu.VMEM((3, 2, 4, GROUP, width), BF16),
            *three(GROUP),
            pltpu.VMEM((3, 2, 4, PAD, width), BF16),
            *three(PAD),
            pltpu.SemaphoreType.DMA((6,)),
            pltpu.SemaphoreType.DMA((REDUCE_SLOTS,)),
            pltpu.SemaphoreType.DMA((REDUCE_SLOTS,)),
        ],
        compiler_params=pltpu.CompilerParams(
            collective_id=1, has_side_effects=True, vmem_limit_bytes=60 * 2**20
        ),
    )(hidden, down_weight[0])
    rows = lax.dynamic_slice(out, (0, 0, 0, ROWS * core, 0), (2, 3, 2, ROWS, width))
    return rows.transpose(3, 1, 0, 2, 4).reshape(ROWS, 12 * width)


def solution(mesh):
    placed = (
        P(("expert", "hidden"), None),
        P(("expert", "hidden"), None),
        P(("expert", "hidden"), None),
        P("expert", None, "hidden"),
        P("expert", None, "hidden"),
        P("expert", "hidden", None),
    )
    return jax.shard_map(
        on_device,
        mesh=mesh,
        in_specs=placed,
        out_specs=P(("expert", "hidden"), None),
        check_vma=False,
    )
```

```python
import jax
import jax.numpy as jnp
from jax import lax
from jax.experimental import pallas as pl
from jax.experimental.pallas import tpu as pltpu
from jax.sharding import PartitionSpec as P

MESH = pl.DeviceIdType.MESH
BF16, F32 = jnp.bfloat16, jnp.float32
ROWS = 12
PARTS = 3
SHARE = ROWS // PARTS
UNIT = 2 * SHARE
GROUP = 4 * UNIT
QUARTER = 4 * GROUP


def hot(axis):
    if isinstance(axis, int):
        return tuple(int(axis == j) for j in range(3))
    return (lax.div((2 - axis) * (1 - axis), 2), axis * (2 - axis), lax.div(axis * (axis - 1), 2))


class Place:
    def __init__(self):
        e, h = lax.axis_index("expert"), lax.axis_index("hidden")
        self.expert = e
        self.core = lax.rem(e, 2)
        self.at = (
            lax.div(h, 8),
            lax.rem(h, 4),
            lax.rem(lax.div(h, 4), 2) * 2 + lax.div(e, 2),
        )

    def device(self, at, core):
        x, y, z = at
        return {
            "expert": lax.rem(z, 2) * 2 + core,
            "hidden": x * 8 + lax.div(z, 2) * 4 + y,
        }

    def sibling(self):
        return self.device(self.at, 1 - self.core)

    def axis(self, p, k):
        return (p + k) % 3 if isinstance(p, int) else lax.rem(p + k, 3)

    def coord(self, p, k):
        return sum(a * o for a, o in zip(self.at, hot(self.axis(p, k))))

    def along(self, p, k, step, other=0):
        on = hot(self.axis(p, k))
        core = 1 - self.core if other else self.core
        return self.device(tuple(lax.rem(a + step * o, 4) for a, o in zip(self.at, on)), core)

def meet(place):
    barrier = pltpu.get_barrier_semaphore()
    partners = [place.sibling()] + [
        place.along(a, 0, step, other) for a in range(3) for step in (1, 2, 3) for other in (0, 1)
    ]
    for partner in partners:
        pl.semaphore_signal(barrier, inc=1, device_id=partner, device_id_type=MESH)
    pl.semaphore_wait(barrier, len(partners))


def each(body):
    pl.loop(0, PARTS)(body)


def plus(i, n):
    return lax.rem(i + n, 4)


class Slots:
    def __init__(self):
        self.count = 0

    def take(self, n):
        base = self.count
        self.count += n
        return base


class Gather:
    def __init__(self, place, wire, slots, k, pick, pieces=1):
        self.place, self.wire, self.k, self.pick, self.pieces = place, wire, k, pick, pieces
        self.base = slots.take(12 + 6 * pieces)

    def own(self, p, half, step):
        ref = self.pick(p, half, self.place.coord(p, self.k))
        slot = self.base + (half * 2 + (0 if step == 1 else 1)) * 3 + p
        return self.wire(slot, ref, ref, self.place.along(p, self.k, step))

    def passed(self, p, half, piece=0):
        ref = self.pick(p, half, plus(self.place.coord(p, self.k), 3 if half == 0 else 1))
        if self.pieces > 1:
            n = ref.shape[0] // self.pieces
            ref = ref.at[pl.ds(piece * n, n)]
        slot = self.base + 12 + (piece * 2 + half) * 3 + p
        return self.wire(slot, ref, ref, self.place.along(p, self.k, 1 if half == 0 else 3))

    def start(self, p):
        self.own(p, 0, 1).start()
        self.own(p, 1, 3).start()
        self.own(p, 1, 1).start()
        self.own(p, 0, 3).start()

    def middle(self, p):
        self.own(p, 0, 1).wait_recv()
        for n in range(self.pieces):
            self.passed(p, 0, n).start()
        self.own(p, 1, 3).wait_recv()
        for n in range(self.pieces):
            self.passed(p, 1, n).start()

    def near(self, p):
        self.own(p, 1, 1).wait_recv()
        self.own(p, 0, 3).wait_recv()

    def far(self, p):
        for n in range(self.pieces):
            self.passed(p, 0, n).wait_recv()
            self.passed(p, 1, n).wait_recv()

    def own_sent(self, p):
        for half in range(2):
            self.own(p, half, 1).wait_send()
            self.own(p, half, 3).wait_send()

    def passed_sent(self, p, half):
        for n in range(self.pieces):
            self.passed(p, half, n).wait_send()


PIECES = 4
SLOTS = 400


def kernel(
    t_ref, c_ref, gate_ref, up_ref, down_ref, out_ref,
    w_ref, wd_ref, first, first_c, x_ref, y_ref, h_ref, table, weight,
    far1, plain1, merged1, z2, got2, z3, got3,
    load_sem, send_sem, recv_sem, credit,
):
    place = Place()
    core, sibling = place.core, place.sibling()
    width = x_ref.shape[-1]
    ff = gate_ref.shape[1]
    block = ff // 2
    slots = Slots()

    def wire(slot, src, dst, device):
        return pltpu.make_async_remote_copy(
            src_ref=src,
            dst_ref=dst,
            send_sem=send_sem.at[slot],
            recv_sem=recv_sem.at[slot],
            device_id=device,
            device_id_type=MESH,
        )

    loads = []
    for n in range(2):
        for m, ref in enumerate((gate_ref, up_ref)):
            loads.append(
                pltpu.make_async_copy(
                    ref.at[:, pl.ds(n * block, block)],
                    w_ref.at[:, pl.ds((2 * n + m) * block, block)],
                    load_sem.at[len(loads)],
                )
            )
    for k in range(4):
        loads.append(
            pltpu.make_async_copy(
                down_ref.at[:, pl.ds(k * width, width)], wd_ref.at[k], load_sem.at[len(loads)]
            )
        )
    for load in loads:
        load.start()
    meet(place)

    base1, base_c = slots.take(24), slots.take(8 + 6)
    others = [(s, o) for s in range(4) for o in range(2) if (s, o) != (0, 0)]

    def dealt(p, s, o):
        to = 1 - core if o else core
        return wire(
            base1 + (2 * s + o) * 3 + p, t_ref.at[to, p], first.at[p, 2 * place.coord(p, 0) + core],
            place.along(p, 0, s, o),
        )

    def dealt_table(s, o):
        at = first_c.at[2 * place.coord(0, 0) + core]
        return wire(base_c + 2 * s + o, c_ref, at, place.along(0, 0, s, o))

    def table_wire(k, s):
        at = table.at[place.coord(0, 2)]
        if k == 1:
            at = at.at[place.coord(0, 1)]
        return wire(base_c + 8 + 3 * (k - 1) + s - 1, at, at, place.along(0, k, s))

    g2 = Gather(
        place, wire, slots, 1,
        lambda p, half, i: x_ref.at[p, 2 * core + half, place.coord(p, 2), i],
    )
    g3 = Gather(
        place, wire, slots, 2, lambda p, half, i: x_ref.at[p, 2 * core + half, i], PIECES
    )
    base_j = slots.take(3 * (5 + 2 * PIECES))

    def joined(p, d, kind, half=None, piece=None):
        i = plus(place.coord(p, 2), d)
        if half is None:
            ref = x_ref.at[p, pl.ds(2 * core, 2), i]
        elif piece is None:
            ref = x_ref.at[p, 2 * core + half, i]
        else:
            n = 4 // PIECES
            ref = x_ref.at[p, 2 * core + half, i, pl.ds(piece * n, n)]
        return wire(base_j + kind * 3 + p, ref, ref, sibling)

    def joined_far(p, half, n):
        return joined(p, 2, 5 + 2 * n + half, half, n)

    def region(p, d, k):
        if d == 0:
            return y_ref.at[p, k]
        return x_ref.at[p, k, plus(place.coord(p, 2), d)]

    base_h, base_r = slots.take(24), slots.take(72)

    def handed(p, d, half):
        return wire(
            base_h + (2 * d + half) * 3 + p, region(p, d, half), region(p, d, 2 + half), sibling
        )

    def quarter(p, d, q, half):
        return region(p, d, 2 + half).at[plus(place.coord(p, 1), q)]

    def ring(p, d, n, q, half, into, step):
        return wire(
            base_r + (6 * d + 2 * n + half) * 3 + p, quarter(p, d, q, half), into.at[d, p, half],
            place.along(p, 1, step),
        )

    def opposite(p, d, half):
        return ring(p, d, 0, 2, half, far1, 1 if half == 0 else 3)

    def direct(p, d, half):
        side = 3 if half == 0 else 1
        return ring(p, d, 1, side, half, plain1, side)

    def relayed(p, d, half):
        side = 1 if half == 0 else 3
        return ring(p, d, 2, side, half, merged1, side)

    base_2, base_3, base_o = slots.take(36), slots.take(9), slots.take(1)

    def second(p, d, s):
        src = z2.at[d, p, plus(place.coord(p, 0), s)]
        return wire(
            base_2 + (3 * d + s - 1) * 3 + p, src, got2.at[d, p, s - 1], place.along(p, 0, s)
        )

    def third(p, d):
        return wire(base_3 + 3 * (d - 1) + p, z3.at[d - 1, p], got3.at[d - 1, p], place.along(p, 2, d))

    last = wire(base_o, out_ref.at[core], out_ref.at[core], sibling)
    assert slots.count <= SLOTS

    def gate_up(d, slot):
        @pl.loop(0, 2)
        def _(n):
            rows = jnp.concatenate(
                [
                    jnp.concatenate(
                        [
                            x_ref[p, k, plus(place.coord(p, 2), d)].reshape(QUARTER, width)
                            for k in range(4)
                        ],
                        axis=1,
                    )
                    for p in range(PARTS)
                ],
                axis=0,
            )
            cols = pl.ds(pl.multiple_of(n * ff, ff), ff)
            result = jnp.dot(rows, w_ref[:, cols], preferred_element_type=F32)
            gate, up = result[:, :block], result[:, block:]
            hidden = gate / (1.0 + jnp.exp(-gate)) * up
            h_ref[slot, :, pl.ds(pl.multiple_of(n * block, block), block)] = hidden.astype(BF16)

    def down(d, slot):
        def scaled(k):
            scale = jnp.concatenate(
                [
                    weight[p, plus(place.coord(p, 2), d)].reshape(QUARTER, 128)
                    for p in range(PARTS)
                ],
                axis=0,
            )
            return jnp.dot(h_ref[slot], wd_ref[k], preferred_element_type=F32) * jnp.concatenate(
                [scale] * (width // 128), axis=1
            )

        for half in range(2):
            result = scaled(2 * (1 - core) + half).astype(BF16)
            for p in range(PARTS):
                region(p, d, half)[...] = result[p * QUARTER : (p + 1) * QUARTER].reshape(
                    4, GROUP, width
                )
            if d and half == 0:
                pl.semaphore_wait(credit.at[d], 1)
            for p in range(PARTS):
                handed(p, d, half).start()
        for half in range(2):
            result = scaled(2 * core + half)
            for p in range(PARTS):
                handed(p, d, half).wait_recv()
                ref = region(p, d, 2 + half)
                mine = result[p * QUARTER : (p + 1) * QUARTER].reshape(4, GROUP, width)
                ref[...] = (mine + ref[...].astype(F32)).astype(BF16)
                opposite(p, d, half).start()
                direct(p, d, half).start()

    def free(d):
        pl.semaphore_signal(credit.at[d], inc=1, device_id=sibling, device_id_type=MESH)

    def merge(d):
        @each
        def _(p):
            for half in range(2):
                opposite(p, d, half).wait_recv()
                ref = quarter(p, d, 1 if half == 0 else 3, half)
                ref[...] = (ref[...].astype(F32) + far1[d, p, half].astype(F32)).astype(BF16)
                relayed(p, d, half).start()

    def total(d):
        @each
        def _(p):
            sums = []
            for half in range(2):
                direct(p, d, half).wait_recv()
                relayed(p, d, half).wait_recv()
                sums.append(
                    quarter(p, d, 0, half)[...].astype(F32)
                    + plain1[d, p, half].astype(F32)
                    + merged1[d, p, half].astype(F32)
                )
            for i in range(4):
                rows = [t[i * UNIT : (i + 1) * UNIT] for t in sums]
                z2[d, p, i] = jnp.concatenate(rows, axis=0).astype(BF16)
            for s in (2, 1, 3):
                second(p, d, s).start()

    def chip_sum(p, d):
        result = z2[d, p, place.coord(p, 0)].astype(F32)
        for s in (1, 2, 3):
            second(p, d, s).wait_recv()
            result = result + got2[d, p, s - 1].astype(F32)
        return result

    for s, o in others:
        for p in range(PARTS):
            dealt(p, s, o).start()
        dealt_table(s, o).start()
    for p in range(PARTS):
        first[p, 2 * place.coord(p, 0) + core] = t_ref[core, p]
    first_c[2 * place.coord(0, 0) + core] = c_ref[...]
    for p in range(PARTS):
        for s, o in others:
            dealt(p, s, o).wait_recv()
        halves = ([], [])
        for i in range(4):
            a, b = first[p, 2 * i].astype(F32), first[p, 2 * i + 1].astype(F32)
            for half in range(2):
                at = half * SHARE
                halves[half].extend([a[at : at + SHARE], b[at : at + SHARE]])
        for half in range(2):
            x_ref[p, 2 * core + half, place.coord(p, 2), place.coord(p, 1)] = jnp.concatenate(
                halves[half], axis=0
            ).astype(BF16)
        g2.start(p)

    for s, o in others:
        dealt_table(s, o).wait_recv()
    table[place.coord(0, 2), place.coord(0, 1)] = sum(first_c[i] for i in range(8))
    for s in (1, 2, 3):
        table_wire(1, s).start()
    each(g2.middle)

    @each
    def _(p):
        g2.near(p)
        g2.far(p)
        g3.start(p)
        joined(p, 0, 0).start()

    for s in (1, 2, 3):
        table_wire(1, s).wait_recv()
    for s in (1, 2, 3):
        table_wire(2, s).start()
    for load in loads[:4]:
        load.wait()
    for p in range(PARTS):
        joined(p, 0, 0).wait_recv()
    gate_up(0, 0)

    @each
    def _(p):
        g3.middle(p)
        joined(p, 3, 1, 0).start()
        joined(p, 1, 2, 1).start()

    for s in (1, 2, 3):
        table_wire(2, s).wait_recv()
    lane = lax.broadcasted_iota(jnp.int32, (UNIT, 128), 1)
    row = lax.broadcasted_iota(jnp.int32, (UNIT, 128), 0)
    token = jnp.where(row < SHARE, row, row - SHARE)

    @pl.loop(0, 16)
    def _(yz):
        y, z = lax.div(yz, 4), lax.rem(yz, 4)
        rows = table[z, y]
        for x in range(4):
            pair = jnp.where(row < SHARE, rows[2 * x : 2 * x + 1], rows[2 * x + 1 : 2 * x + 2])
            at = (x, y, z)
            for p in range(PARTS):
                chosen = lane == (token + p * SHARE) * 4 + place.expert
                value = jnp.sum(jnp.where(chosen, pair, 0.0), axis=1, keepdims=True)
                weight[p, at[(p + 2) % 3], at[(p + 1) % 3], at[p]] = jnp.broadcast_to(
                    value, (UNIT, 128)
                )

    for load in loads[4:]:
        load.wait()
    down(0, 0)

    @each
    def _(p):
        g3.near(p)
        joined(p, 3, 3, 1).start()
        joined(p, 1, 4, 0).start()

    for p in range(PARTS):
        joined(p, 3, 1, 0).wait_recv()
        joined(p, 3, 3, 1).wait_recv()
    gate_up(3, 0)
    merge(0)
    for p in range(PARTS):
        joined(p, 1, 2, 1).wait_recv()
        joined(p, 1, 4, 0).wait_recv()
    gate_up(1, 1)

    @each
    def _(p):
        g3.passed_sent(p, 0)
        joined(p, 3, 1, 0).wait_send()
        joined(p, 3, 3, 1).wait_send()

    free(3)
    down(3, 0)

    @each
    def _(p):
        for n in range(PIECES):
            for half in range(2):
                g3.passed(p, half, n).wait_recv()
                joined_far(p, half, n).start()
        g3.passed_sent(p, 1)
        joined(p, 1, 2, 1).wait_send()
        joined(p, 1, 4, 0).wait_send()

    free(1)
    down(1, 1)
    merge(3)

    @each
    def _(p):
        for n in range(PIECES):
            for half in range(2):
                joined_far(p, half, n).wait_recv()

    gate_up(2, 0)

    @each
    def _(p):
        for n in range(PIECES):
            for half in range(2):
                joined_far(p, half, n).wait_send()

    free(2)
    merge(1)
    total(0)
    down(2, 0)
    total(3)
    merge(2)
    total(1)

    def finish(d):
        @each
        def _(p):
            z3[d - 1, p] = chip_sum(p, d).astype(BF16)
            third(p, d).start()

    finish(3)
    finish(1)
    total(2)
    finish(2)

    @each
    def _(p):
        result = chip_sum(p, 0)
        for d in (3, 1, 2):
            third(p, d).wait_recv()
            result = result + got3[d - 1, p].astype(F32)
        out_ref[core, p] = result.astype(BF16)

    last.start()

    for s, o in others:
        dealt_table(s, o).wait_send()
    for k in (1, 2):
        for s in (1, 2, 3):
            table_wire(k, s).wait_send()

    @each
    def _(p):
        for s, o in others:
            dealt(p, s, o).wait_send()
        g2.own_sent(p)
        g2.passed_sent(p, 0)
        g2.passed_sent(p, 1)
        g3.own_sent(p)
        joined(p, 0, 0).wait_send()
        for d in range(4):
            for half in range(2):
                handed(p, d, half).wait_send()
                opposite(p, d, half).wait_send()
                direct(p, d, half).wait_send()
                relayed(p, d, half).wait_send()
            for s in (1, 2, 3):
                second(p, d, s).wait_send()
            if d:
                third(p, d).wait_send()

    last.wait_recv()
    last.wait_send()


def on_device(tokens, routes, combine, gate_weight, up_weight, down_weight):
    model_width = tokens.shape[1]
    width = model_width // 4
    ff = gate_weight.shape[2]
    place = Place()
    core = place.core
    shares = (
        tokens.reshape(PARTS, SHARE, 2, 2, width)
        .transpose(2, 0, 3, 1, 4)
        .reshape(2, PARTS, 2 * SHARE, width)
    )
    experts = jnp.arange(4, dtype=jnp.int32)
    dense = jnp.sum(
        jnp.where(routes[:, :, None] == experts, combine[:, :, None], 0.0), axis=1
    ).reshape(1, 4 * ROWS)
    dense = jnp.pad(dense, ((0, 0), (0, 128 - 4 * ROWS)))
    mine = jnp.arange(8, dtype=jnp.int32)[:, None] == 2 * place.at[0] + core
    dense = jnp.where(mine, dense, 0.0)

    vmem = pl.BlockSpec(memory_space=pltpu.VMEM)
    hbm = pl.BlockSpec(memory_space=pl.ANY)

    def ring_buffer():
        return pltpu.VMEM((4, PARTS, 2, GROUP, width), BF16)

    out = pl.pallas_call(
        kernel,
        out_shape=jax.ShapeDtypeStruct((2, PARTS, 2 * UNIT, width), BF16),
        in_specs=[vmem, vmem, hbm, hbm, hbm],
        out_specs=vmem,
        scratch_shapes=[
            pltpu.VMEM((model_width, 2 * ff), BF16),
            pltpu.VMEM((4, ff, width), BF16),
            pltpu.VMEM((PARTS, 8, 2 * SHARE, width), BF16),
            pltpu.VMEM((8, 8, 128), F32),
            pltpu.VMEM((PARTS, 4, 4, 4, GROUP, width), BF16),
            pltpu.VMEM((PARTS, 4, 4, GROUP, width), BF16),
            pltpu.VMEM((2, PARTS * QUARTER, ff), BF16),
            pltpu.VMEM((4, 4, 8, 128), F32),
            pltpu.VMEM((PARTS, 4, 4, 4, UNIT, 128), F32),
            ring_buffer(),
            ring_buffer(),
            ring_buffer(),
            pltpu.VMEM((4, PARTS, 4, 2 * UNIT, width), BF16),
            pltpu.VMEM((4, PARTS, 3, 2 * UNIT, width), BF16),
            pltpu.VMEM((3, PARTS, 2 * UNIT, width), BF16),
            pltpu.VMEM((3, PARTS, 2 * UNIT, width), BF16),
            pltpu.SemaphoreType.DMA((8,)),
            pltpu.SemaphoreType.DMA((SLOTS,)),
            pltpu.SemaphoreType.DMA((SLOTS,)),
            pltpu.SemaphoreType.REGULAR((4,)),
        ],
        compiler_params=pltpu.CompilerParams(
            collective_id=0, has_side_effects=True, vmem_limit_bytes=62 * 2**20
        ),
    )(shares, dense, gate_weight[0], up_weight[0], down_weight[0])
    rows = out.reshape(2, PARTS, 2, 2, SHARE, width)
    rows = lax.dynamic_index_in_dim(rows, core, axis=3, keepdims=False)
    return rows.transpose(1, 3, 0, 2, 4).reshape(ROWS, model_width)


def solution(mesh):
    placed = (
        P(("expert", "hidden"), None),
        P(("expert", "hidden"), None),
        P(("expert", "hidden"), None),
        P("expert", None, "hidden"),
        P("expert", None, "hidden"),
        P("expert", "hidden", None),
    )
    return jax.shard_map(
        on_device,
        mesh=mesh,
        in_specs=placed,
        out_specs=P(("expert", "hidden"), None),
        check_vma=False,
    )
```

```python
import jax
import jax.numpy as jnp
from jax import lax
from jax.experimental import pallas as pl
from jax.experimental.pallas import tpu as pltpu
from jax.sharding import PartitionSpec as P

MESH = pl.DeviceIdType.MESH
BF16, F32 = jnp.bfloat16, jnp.float32
ROWS = 12
PARTS = 3
SHARE = ROWS // PARTS
UNIT = 2 * SHARE
GROUP = 4 * UNIT
QUARTER = 4 * GROUP


def hot(axis):
    if isinstance(axis, int):
        return tuple(int(axis == j) for j in range(3))
    return (lax.div((2 - axis) * (1 - axis), 2), axis * (2 - axis), lax.div(axis * (axis - 1), 2))


class Place:
    def __init__(self):
        e, h = lax.axis_index("expert"), lax.axis_index("hidden")
        self.expert = e
        self.core = lax.rem(e, 2)
        self.at = (
            lax.div(h, 8),
            lax.rem(h, 4),
            lax.rem(lax.div(h, 4), 2) * 2 + lax.div(e, 2),
        )

    def device(self, at, core):
        x, y, z = at
        return {
            "expert": lax.rem(z, 2) * 2 + core,
            "hidden": x * 8 + lax.div(z, 2) * 4 + y,
        }

    def sibling(self):
        return self.device(self.at, 1 - self.core)

    def axis(self, p, k):
        return (p + k) % 3 if isinstance(p, int) else lax.rem(p + k, 3)

    def coord(self, p, k):
        return sum(a * o for a, o in zip(self.at, hot(self.axis(p, k))))

    def along(self, p, k, step, other=0):
        on = hot(self.axis(p, k))
        core = 1 - self.core if other else self.core
        return self.device(tuple(lax.rem(a + step * o, 4) for a, o in zip(self.at, on)), core)

def meet(place):
    barrier = pltpu.get_barrier_semaphore()
    partners = [place.sibling()] + [
        place.along(a, 0, step, other) for a in range(3) for step in (1, 2, 3) for other in (0, 1)
    ]
    for partner in partners:
        pl.semaphore_signal(barrier, inc=1, device_id=partner, device_id_type=MESH)
    pl.semaphore_wait(barrier, len(partners))


def each(body):
    pl.loop(0, PARTS)(body)


def plus(i, n):
    return lax.rem(i + n, 4)


class Slots:
    def __init__(self):
        self.count = 0

    def take(self, n):
        base = self.count
        self.count += n
        return base


SENDS, RECVS = 24, 96


def kernel(
    tok_ref, route_ref, comb_ref, gate_ref, up_ref, down_ref, out_ref,
    w_ref, wd_ref, t_ref, c_ref, pad_c, pad_r, first, first_c, x_ref, y_ref, h_ref, table, weight,
    far1, plain1, merged1, z2, got2, z3, got3, o_ref,
    load_sem, send_sem, recv_sem, credit,
):
    place = Place()
    core, sibling = place.core, place.sibling()
    width = x_ref.shape[-1]
    ff = gate_ref.shape[1]
    block = ff // 2
    sends, recvs = Slots(), Slots()

    def wire(send, recv, src, dst, device):
        return pltpu.make_async_remote_copy(
            src_ref=src,
            dst_ref=dst,
            send_sem=send_sem.at[send],
            recv_sem=recv_sem.at[recv],
            device_id=device,
            device_id_type=MESH,
        )

    def sent(slot, ref):
        wire(slot, 0, ref, ref, sibling).wait_send()

    def arrived(slot, ref):
        wire(0, slot, ref, ref, sibling).wait_recv()

    loads = []
    for n in range(2):
        for m, ref in enumerate((gate_ref, up_ref)):
            loads.append(
                pltpu.make_async_copy(
                    ref.at[:, pl.ds(n * block, block)],
                    w_ref.at[:, pl.ds((2 * n + m) * block, block)],
                    load_sem.at[len(loads)],
                )
            )
    for k in range(4):
        loads.append(
            pltpu.make_async_copy(
                down_ref.at[:, pl.ds(k * width, width)], wd_ref.at[k], load_sem.at[len(loads)]
            )
        )

    for k in range(4):
        rows = tok_ref[:, k * width : (k + 1) * width].astype(F32)
        for p in range(PARTS):
            at = (k % 2) * SHARE
            t_ref[k // 2, p, at : at + SHARE] = rows[p * SHARE : (p + 1) * SHARE].astype(BF16)
    pad_c[...] = jnp.zeros(pad_c.shape, F32)
    pad_r[...] = jnp.zeros(pad_r.shape, jnp.int32)
    pad_c[0:2, 0:ROWS] = comb_ref[...]
    pad_r[0:2, 0:ROWS] = route_ref[...]
    spread = pad_c[...] * 0.0
    for e in range(4):
        mine = jnp.where(pad_r[...] == e, pad_c[...], 0.0)
        spread = spread + (pltpu.roll(mine, 16 * e, 1) if e else mine)
    c_ref[...] = jnp.broadcast_to(jnp.sum(spread, axis=0, keepdims=True), (8, 128))

    meet(place)

    others = [(s, o) for s in (0, 1, 3, 2) for o in range(2) if (s, o) != (0, 0)]
    s_deal, r_deal = sends.take(1), recvs.take(3)
    s_table, r_table = sends.take(3), recvs.take(3)

    def dealt(p, s, o):
        to = 1 - core if o else core
        return wire(
            s_deal, r_deal + p, t_ref.at[to, p], first.at[p, 2 * ((4 - s) % 4) + core],
            place.along(p, 0, s, o),
        )

    def dealt_table(s, o):
        at = first_c.at[2 * ((4 - s) % 4) + core]
        return wire(s_table, r_table, c_ref, at, place.along(0, 0, s, o))

    def table_wire(k, s):
        if k == 1:
            src, dst = table.at[0, 0], table.at[0, 4 - s]
        else:
            src, dst = table.at[0], table.at[4 - s]
        return wire(s_table + k, r_table + k, src, dst, place.along(0, k, s))

    s_two, r_two = sends.take(2), recvs.take(9)

    def two(p, half, step):
        at = x_ref.at[p, 2 * core + half, 0]
        kind = 0 if half == (0 if step == 1 else 1) else 2
        slot = r_two + (half if kind == 0 else 2) * 3 + p
        return wire(s_two, slot, at.at[0], at.at[4 - step], place.along(p, 1, step))

    def two_on(p, half):
        at = x_ref.at[p, 2 * core + half, 0]
        step = 1 if half == 0 else 3
        return wire(s_two + 1, r_two + 6 + p, at.at[4 - step], at.at[2], place.along(p, 1, step))

    s_three, r_three = sends.take(3), recvs.take(9 + 12)

    def three(p, half, step, rest):
        at = x_ref.at[p, 2 * core + half]
        groups = pl.ds(1, 3) if rest else pl.ds(0, 1)
        kind = half if half == (0 if step == 1 else 1) else 2
        return wire(
            s_three, r_three + kind * 3 + p, at.at[0, groups], at.at[4 - step, groups],
            place.along(p, 2, step),
        )

    def three_all(p, rest):
        for half, step in ((0, 1), (1, 3), (1, 1), (0, 3)):
            three(p, half, step, rest).start()

    def three_on(p, half, g):
        at = x_ref.at[p, 2 * core + half]
        step = 1 if half == 0 else 3
        return wire(
            s_three + 1 + half, r_three + 9 + 3 * g + p, at.at[4 - step, g], at.at[2, g],
            place.along(p, 2, step),
        )

    s_join, r_join = sends.take(4), recvs.take(4)

    def joined(p, d, half=None, g=None):
        if half is None:
            ref = x_ref.at[p, pl.ds(2 * core, 2), d]
        else:
            ref = x_ref.at[p, 2 * core + half, d]
        if g is not None:
            ref = ref.at[g]
        return wire(s_join + d, r_join + d, ref, ref, sibling)

    half_of_quarter = x_ref.at[:, pl.ds(0, 2), 0]

    def region(p, d, k):
        if d == 0:
            return y_ref.at[p, k]
        return x_ref.at[p, k, {3: 0, 1: 3, 2: 1}[d]]

    s_hand, r_hand = sends.take(1), recvs.take(8)

    def handed(p, d, half):
        return wire(
            s_hand, r_hand + 2 * d + half, region(p, d, half), region(p, d, 2 + half), sibling
        )

    s_ring, r_ring = sends.take(3), recvs.take(24)

    def ring(p, d, n, q, half, into, step):
        slot = r_ring + 3 * d + p + (12 if n else 0)
        return wire(
            s_ring + n, slot, region(p, d, 2 + half).at[q], into.at[d, p, half],
            place.along(p, 1, step),
        )

    def opposite(p, d, half):
        return ring(p, d, 0, 2, half, far1, 1 if half == 0 else 3)

    def direct(p, d, half):
        side = 3 if half == 0 else 1
        return ring(p, d, 1, side, half, plain1, side)

    def relayed(p, d, half):
        side = 1 if half == 0 else 3
        return ring(p, d, 2, side, half, merged1, side)

    s_second, r_second = sends.take(1), recvs.take(12)
    s_third, r_third = sends.take(1), recvs.take(3)
    s_last, r_last = sends.take(1), recvs.take(1)
    assert sends.count <= SENDS and recvs.count <= RECVS

    def second(p, d, s):
        return wire(
            s_second, r_second + 3 * d + p, z2.at[d, p, s], got2.at[d, p, s - 1],
            place.along(p, 0, s),
        )

    def third(p, d):
        return wire(
            s_third, r_third + p, z3.at[d - 1, p], got3.at[d - 1, p], place.along(p, 2, d)
        )

    last = wire(s_last, r_last, o_ref.at[core], o_ref.at[core], sibling)

    def gate_up(d):
        @pl.loop(0, 2)
        def _(n):
            rows = jnp.concatenate(
                [
                    jnp.concatenate(
                        [x_ref[p, k, d].reshape(QUARTER, width) for k in range(4)], axis=1
                    )
                    for p in range(PARTS)
                ],
                axis=0,
            )
            cols = pl.ds(pl.multiple_of(n * ff, ff), ff)
            result = jnp.dot(rows, w_ref[:, cols], preferred_element_type=F32)
            gate, up = result[:, :block], result[:, block:]
            hidden = gate / (1.0 + jnp.exp(-gate)) * up
            h_ref[:, pl.ds(pl.multiple_of(n * block, block), block)] = hidden.astype(BF16)

    def down(d):
        def scaled(k):
            scale = jnp.concatenate(
                [weight[p, d].reshape(QUARTER, 128) for p in range(PARTS)], axis=0
            )
            return jnp.dot(h_ref[...], wd_ref[k], preferred_element_type=F32) * jnp.concatenate(
                [scale] * (width // 128), axis=1
            )

        for half in range(2):
            result = scaled(2 * (1 - core) + half).astype(BF16)
            for p in range(PARTS):
                region(p, d, half)[...] = result[p * QUARTER : (p + 1) * QUARTER].reshape(
                    4, GROUP, width
                )
            if d and half == 0:
                pl.semaphore_wait(credit.at[d], 1)
            for p in range(PARTS):
                handed(p, d, half).start()
        for half in range(2):
            result = scaled(2 * core + half)
            arrived(r_hand + 2 * d + half, x_ref.at[0, pl.ds(0, 3), 0])
            for p in range(PARTS):
                ref = region(p, d, 2 + half)
                mine = result[p * QUARTER : (p + 1) * QUARTER].reshape(4, GROUP, width)
                ref[...] = (mine + ref[...].astype(F32)).astype(BF16)
                opposite(p, d, half).start()
                direct(p, d, half).start()

    def free(d):
        pl.semaphore_signal(credit.at[d], inc=1, device_id=sibling, device_id_type=MESH)

    def merge(d):
        @each
        def _(p):
            arrived(r_ring + 3 * d + p, far1.at[d, p])
            for half in range(2):
                ref = region(p, d, 2 + half).at[1 if half == 0 else 3]
                ref[...] = (ref[...].astype(F32) + far1[d, p, half].astype(F32)).astype(BF16)
                relayed(p, d, half).start()

    def total(d):
        @each
        def _(p):
            arrived(r_ring + 12 + 3 * d + p, x_ref.at[0, 0, 0])
            sums = [
                region(p, d, 2 + half)[0].astype(F32)
                + plain1[d, p, half].astype(F32)
                + merged1[d, p, half].astype(F32)
                for half in range(2)
            ]
            for i in range(4):
                rows = [t[i * UNIT : (i + 1) * UNIT] for t in sums]
                z2[d, p, i] = jnp.concatenate(rows, axis=0).astype(BF16)
            for s in (2, 1, 3):
                second(p, d, s).start()

    def chip_sum(p, d):
        arrived(r_second + 3 * d + p, got2.at[d, p])
        result = z2[d, p, 0].astype(F32)
        for s in (1, 2, 3):
            result = result + got2[d, p, s - 1].astype(F32)
        return result

    for s, o in others:
        for p in range(PARTS):
            dealt(p, s, o).start()
    for s, o in others:
        dealt_table(s, o).start()
    for load in loads:
        load.start()
    for p in range(PARTS):
        first[p, core] = t_ref[core, p]
    first_c[core] = c_ref[...]
    for p in range(PARTS):
        arrived(r_deal + p, first.at[p, pl.ds(0, 7)])
        halves = ([], [])
        for i in range(4):
            a, b = first[p, 2 * i].astype(F32), first[p, 2 * i + 1].astype(F32)
            for half in range(2):
                at = half * SHARE
                halves[half].extend([a[at : at + SHARE], b[at : at + SHARE]])
        for half in range(2):
            x_ref[p, 2 * core + half, 0, 0] = jnp.concatenate(halves[half], axis=0).astype(BF16)
        for half, step in ((0, 1), (1, 3), (1, 1), (0, 3)):
            two(p, half, step).start()
        three_all(p, False)

    arrived(r_table, first_c.at[pl.ds(0, 7)])
    row8 = lax.broadcasted_iota(jnp.int32, (8, 128), 0)
    table[0, 0] = sum(jnp.where(row8 == i, first_c[i], 0.0) for i in range(8))
    for s in (1, 2, 3):
        table_wire(1, s).start()

    @each
    def _(p):
        for half in range(2):
            arrived(r_two + 3 * half + p, x_ref.at[0, 0, 0, 0])
            two_on(p, half).start()

    @each
    def _(p):
        arrived(r_two + 6 + p, x_ref.at[0, 0, 0])
        three_all(p, True)
        joined(p, 0).start()

    arrived(r_table + 1, first_c.at[pl.ds(0, 3)])
    for s in (1, 2, 3):
        table_wire(2, s).start()
    for load in loads[:4]:
        load.wait()
    arrived(r_join, half_of_quarter)
    gate_up(0)

    arrived(r_table + 2, table.at[pl.ds(0, 3)])
    lane = lax.broadcasted_iota(jnp.int32, (UNIT, 128), 1)
    row = lax.broadcasted_iota(jnp.int32, (UNIT, 128), 0)
    token = jnp.where(row < SHARE, row, row - SHARE) + place.expert * 16

    @pl.loop(0, 16)
    def _(yz):
        y, z = lax.div(yz, 4), lax.rem(yz, 4)
        rows = table[z, y]
        for x in range(4):
            pair = jnp.where(row < SHARE, rows[2 * x : 2 * x + 1], rows[2 * x + 1 : 2 * x + 2])
            at = (x, y, z)
            for p in range(PARTS):
                chosen = lane == token + p * SHARE
                value = jnp.sum(jnp.where(chosen, pair, 0.0), axis=1, keepdims=True)
                weight[p, at[(p + 2) % 3], at[(p + 1) % 3], at[p]] = jnp.broadcast_to(
                    value, (UNIT, 128)
                )

    for load in loads[4:]:
        load.wait()
    down(0)

    @each
    def _(p):
        for half in range(2):
            arrived(r_three + 3 * half + p, x_ref.at[0, 0, 0])
            for g in range(4):
                three_on(p, half, g).start()
            joined(p, 3 if half == 0 else 1, half).start()

    @each
    def _(p):
        arrived(r_three + 6 + p, x_ref.at[0, pl.ds(0, 2), 0])
        joined(p, 3, 1).start()
        joined(p, 1, 0).start()

    sent(s_two, x_ref.at[:, :, 0, 0])
    sent(s_two + 1, far1.at[0])
    sent(s_three, x_ref.at[:, :, 0])
    sent(s_join, half_of_quarter)
    free(3)
    arrived(r_join + 3, half_of_quarter)
    gate_up(3)
    merge(0)
    down(3)
    arrived(r_join + 1, half_of_quarter)
    gate_up(1)

    @each
    def _(p):
        for g in range(4):
            arrived(r_three + 9 + 3 * g + p, x_ref.at[0, 0, 0, pl.ds(0, 2)])
            for half in range(2):
                joined(p, 2, half, g).start()

    sent(s_three + 1, x_ref.at[:, 0, 0])
    sent(s_join + 3, half_of_quarter)
    free(1)
    sent(s_three + 2, x_ref.at[:, 0, 0])
    sent(s_join + 1, half_of_quarter)
    free(2)
    merge(3)
    down(1)
    arrived(r_join + 2, half_of_quarter)
    gate_up(2)
    merge(1)
    total(0)
    down(2)
    total(3)
    merge(2)
    total(1)

    def finish(d):
        @each
        def _(p):
            z3[d - 1, p] = chip_sum(p, d).astype(BF16)
            third(p, d).start()

    finish(3)
    finish(1)
    total(2)
    finish(2)

    @each
    def _(p):
        result = chip_sum(p, 0)
        arrived(r_third + p, got3.at[:, 0])
        for d in (3, 1, 2):
            result = result + got3[d - 1, p].astype(F32)
        o_ref[core, p] = result.astype(BF16)

    last.start()

    sent(s_deal, first.at[:, pl.ds(0, 7)])
    sent(s_table, first_c.at[pl.ds(0, 7)])
    sent(s_table + 1, first_c.at[pl.ds(0, 3)])
    sent(s_table + 2, table.at[pl.ds(0, 3)])
    sent(s_join + 2, half_of_quarter)
    sent(s_hand, x_ref.at[:, pl.ds(0, 2)])
    sent(s_ring, far1)
    sent(s_ring + 1, far1)
    sent(s_ring + 2, far1)
    sent(s_second, got2)
    sent(s_third, got3)
    last.wait_recv()
    for k in range(4):
        rows = []
        for p in range(PARTS):
            both = o_ref[k // 2, p].astype(F32)
            at = (k % 2) * UNIT
            rows.append(
                jnp.where(core == 0, both[at : at + SHARE], both[at + SHARE : at + 2 * SHARE])
            )
        out_ref[:, k * width : (k + 1) * width] = jnp.concatenate(rows, axis=0).astype(BF16)
    last.wait_send()


def on_device(tokens, routes, combine, gate_weight, up_weight, down_weight):
    model_width = tokens.shape[1]
    width = model_width // 4
    ff = gate_weight.shape[2]
    vmem = pl.BlockSpec(memory_space=pltpu.VMEM)
    hbm = pl.BlockSpec(memory_space=pl.ANY)

    def ring_buffer():
        return pltpu.VMEM((4, PARTS, 2, GROUP, width), BF16)

    return pl.pallas_call(
        kernel,
        out_shape=jax.ShapeDtypeStruct((ROWS, model_width), BF16),
        in_specs=[vmem, vmem, vmem, hbm, hbm, hbm],
        out_specs=vmem,
        scratch_shapes=[
            pltpu.VMEM((model_width, 2 * ff), BF16),
            pltpu.VMEM((4, ff, width), BF16),
            pltpu.VMEM((2, PARTS, 2 * SHARE, width), BF16),
            pltpu.VMEM((8, 128), F32),
            pltpu.VMEM((8, 128), F32),
            pltpu.VMEM((8, 128), jnp.int32),
            pltpu.VMEM((PARTS, 8, 2 * SHARE, width), BF16),
            pltpu.VMEM((8, 8, 128), F32),
            pltpu.VMEM((PARTS, 4, 4, 4, GROUP, width), BF16),
            pltpu.VMEM((PARTS, 4, 4, GROUP, width), BF16),
            pltpu.VMEM((PARTS * QUARTER, ff), BF16),
            pltpu.VMEM((4, 4, 8, 128), F32),
            pltpu.VMEM((PARTS, 4, 4, 4, UNIT, 128), F32),
            ring_buffer(),
            ring_buffer(),
            ring_buffer(),
            pltpu.VMEM((4, PARTS, 4, 2 * UNIT, width), BF16),
            pltpu.VMEM((4, PARTS, 3, 2 * UNIT, width), BF16),
            pltpu.VMEM((3, PARTS, 2 * UNIT, width), BF16),
            pltpu.VMEM((3, PARTS, 2 * UNIT, width), BF16),
            pltpu.VMEM((2, PARTS, 2 * UNIT, width), BF16),
            pltpu.SemaphoreType.DMA((8,)),
            pltpu.SemaphoreType.DMA((SENDS,)),
            pltpu.SemaphoreType.DMA((RECVS,)),
            pltpu.SemaphoreType.REGULAR((4,)),
        ],
        compiler_params=pltpu.CompilerParams(
            collective_id=0, has_side_effects=True, vmem_limit_bytes=62 * 2**20
        ),
    )(tokens, routes.T, combine.T, gate_weight[0], up_weight[0], down_weight[0])


def solution(mesh):
    placed = (
        P(("expert", "hidden"), None),
        P(("expert", "hidden"), None),
        P(("expert", "hidden"), None),
        P("expert", None, "hidden"),
        P("expert", None, "hidden"),
        P("expert", "hidden", None),
    )
    return jax.shard_map(
        on_device,
        mesh=mesh,
        in_specs=placed,
        out_specs=P(("expert", "hidden"), None),
        check_vma=False,
    )
```

```python
import jax
import jax.numpy as jnp
from jax import lax
from jax.experimental import pallas as pl
from jax.experimental.pallas import tpu as pltpu
from jax.sharding import PartitionSpec as P

MESH = pl.DeviceIdType.MESH
BF16, F32 = jnp.bfloat16, jnp.float32
ROWS = 12
PARTS = 3
SHARE = ROWS // PARTS
UNIT = 2 * SHARE
GROUP = 4 * UNIT
QUARTER = 4 * GROUP


def hot(axis):
    if isinstance(axis, int):
        return tuple(int(axis == j) for j in range(3))
    return (lax.div((2 - axis) * (1 - axis), 2), axis * (2 - axis), lax.div(axis * (axis - 1), 2))


class Place:
    def __init__(self):
        e, h = lax.axis_index("expert"), lax.axis_index("hidden")
        self.expert = e
        self.core = lax.rem(e, 2)
        self.at = (
            lax.div(h, 8),
            lax.rem(h, 4),
            lax.rem(lax.div(h, 4), 2) * 2 + lax.div(e, 2),
        )

    def device(self, at, core):
        x, y, z = at
        return {
            "expert": lax.rem(z, 2) * 2 + core,
            "hidden": x * 8 + lax.div(z, 2) * 4 + y,
        }

    def sibling(self):
        return self.device(self.at, 1 - self.core)

    def axis(self, p, k):
        return (p + k) % 3 if isinstance(p, int) else lax.rem(p + k, 3)

    def coord(self, p, k):
        return sum(a * o for a, o in zip(self.at, hot(self.axis(p, k))))

    def along(self, p, k, step, other=0):
        on = hot(self.axis(p, k))
        core = 1 - self.core if other else self.core
        return self.device(tuple(lax.rem(a + step * o, 4) for a, o in zip(self.at, on)), core)

def meet(place):
    barrier = pltpu.get_barrier_semaphore()
    partners = [place.sibling()] + [
        place.along(a, 0, step, other) for a in range(3) for step in (1, 2, 3) for other in (0, 1)
    ]
    for partner in partners:
        pl.semaphore_signal(barrier, inc=1, device_id=partner, device_id_type=MESH)
    pl.semaphore_wait(barrier, len(partners))


def each(body):
    pl.loop(0, PARTS)(body)


def plus(i, n):
    return lax.rem(i + n, 4)


class Slots:
    def __init__(self):
        self.count = 0

    def take(self, n):
        base = self.count
        self.count += n
        return base


SENDS, RECVS = 24, 96


def kernel(
    tok_ref, route_ref, comb_ref, gate_ref, up_ref, down_ref, out_ref,
    w_ref, wd_ref, t_ref, c_ref, pad_c, pad_r, first, first_c, x_ref, y_ref, h_ref, table, weight,
    far1, plain1, merged1, z2, got2, z3, got3, o_ref,
    load_sem, send_sem, recv_sem, credit,
):
    place = Place()
    core, sibling = place.core, place.sibling()
    width = x_ref.shape[-1]
    ff = gate_ref.shape[1]
    block = ff // 2
    sends, recvs = Slots(), Slots()

    def wire(send, recv, src, dst, device):
        return pltpu.make_async_remote_copy(
            src_ref=src,
            dst_ref=dst,
            send_sem=send_sem.at[send],
            recv_sem=recv_sem.at[recv],
            device_id=device,
            device_id_type=MESH,
        )

    def sent(slot, ref):
        wire(slot, 0, ref, ref, sibling).wait_send()

    def arrived(slot, ref):
        wire(0, slot, ref, ref, sibling).wait_recv()

    loads = []
    for n in range(2):
        for m, ref in enumerate((gate_ref, up_ref)):
            loads.append(
                pltpu.make_async_copy(
                    ref.at[:, pl.ds(n * block, block)],
                    w_ref.at[:, pl.ds((2 * n + m) * block, block)],
                    load_sem.at[len(loads)],
                )
            )
    for k in range(4):
        loads.append(
            pltpu.make_async_copy(
                down_ref.at[:, pl.ds(k * width, width)], wd_ref.at[k], load_sem.at[len(loads)]
            )
        )

    for k in range(4):
        rows = tok_ref[:, k * width : (k + 1) * width].astype(F32)
        for p in range(PARTS):
            at = (k % 2) * SHARE
            t_ref[k // 2, p, at : at + SHARE] = rows[p * SHARE : (p + 1) * SHARE].astype(BF16)
    pad_c[...] = jnp.zeros(pad_c.shape, F32)
    pad_r[...] = jnp.zeros(pad_r.shape, jnp.int32)
    pad_c[0:2, 0:ROWS] = comb_ref[...]
    pad_r[0:2, 0:ROWS] = route_ref[...]
    spread = pad_c[...] * 0.0
    for e in range(4):
        mine = jnp.where(pad_r[...] == e, pad_c[...], 0.0)
        spread = spread + (pltpu.roll(mine, 16 * e, 1) if e else mine)
    c_ref[...] = jnp.broadcast_to(jnp.sum(spread, axis=0, keepdims=True), (8, 128))

    meet(place)

    others = [(s, o) for s in (0, 1, 3, 2) for o in range(2) if (s, o) != (0, 0)]
    s_deal, r_deal = sends.take(1), recvs.take(3)
    s_table, r_table = sends.take(3), recvs.take(3)

    def dealt(p, s, o):
        to = 1 - core if o else core
        return wire(
            s_deal, r_deal + p, t_ref.at[to, p], first.at[p, 2 * ((4 - s) % 4) + core],
            place.along(p, 0, s, o),
        )

    def dealt_table(s, o):
        at = first_c.at[2 * ((4 - s) % 4) + core]
        return wire(s_table, r_table, c_ref, at, place.along(0, 0, s, o))

    def table_wire(k, s):
        if k == 1:
            src, dst = table.at[0, 0], table.at[0, 4 - s]
        else:
            src, dst = table.at[0], table.at[4 - s]
        return wire(s_table + k, r_table + k, src, dst, place.along(0, k, s))

    s_two, r_two = sends.take(2), recvs.take(9)

    def two(p, half, step):
        at = x_ref.at[p, 2 * core + half, 0]
        kind = 0 if half == (0 if step == 1 else 1) else 2
        slot = r_two + (half if kind == 0 else 2) * 3 + p
        return wire(s_two, slot, at.at[0], at.at[4 - step], place.along(p, 1, step))

    def two_on(p, half):
        at = x_ref.at[p, 2 * core + half, 0]
        step = 1 if half == 0 else 3
        return wire(s_two + 1, r_two + 6 + p, at.at[4 - step], at.at[2], place.along(p, 1, step))

    s_three, r_three = sends.take(3), recvs.take(9 + 12)

    def three(p, half, step, rest):
        at = x_ref.at[p, 2 * core + half]
        groups = pl.ds(1, 3) if rest else pl.ds(0, 1)
        kind = half if half == (0 if step == 1 else 1) else 2
        return wire(
            s_three, r_three + kind * 3 + p, at.at[0, groups], at.at[4 - step, groups],
            place.along(p, 2, step),
        )

    def three_all(p, rest):
        for half, step in ((0, 1), (1, 3), (1, 1), (0, 3)):
            three(p, half, step, rest).start()

    def three_on(p, half, g):
        at = x_ref.at[p, 2 * core + half]
        step = 1 if half == 0 else 3
        return wire(
            s_three + 1 + half, r_three + 9 + 3 * g + p, at.at[4 - step, g], at.at[2, g],
            place.along(p, 2, step),
        )

    s_join, r_join = sends.take(4), recvs.take(4)

    def joined(p, d, half=None, g=None):
        if half is None:
            ref = x_ref.at[p, pl.ds(2 * core, 2), d]
        else:
            ref = x_ref.at[p, 2 * core + half, d]
        if g is not None:
            ref = ref.at[g]
        return wire(s_join + d, r_join + d, ref, ref, sibling)

    half_of_quarter = x_ref.at[:, pl.ds(0, 2), 0]

    def region(p, d, k):
        if d == 0:
            return y_ref.at[p, k]
        return x_ref.at[p, k, {3: 0, 1: 3, 2: 1}[d]]

    s_hand, r_hand = sends.take(1), recvs.take(8)

    def handed(p, d, half):
        return wire(
            s_hand, r_hand + 2 * d + half, region(p, d, half), region(p, d, 2 + half), sibling
        )

    s_ring, r_ring = sends.take(3), recvs.take(24)

    def ring(p, d, n, q, half, into, step):
        slot = r_ring + 3 * d + p + (12 if n else 0)
        return wire(
            s_ring + n, slot, region(p, d, 2 + half).at[q], into.at[d, p, half],
            place.along(p, 1, step),
        )

    def opposite(p, d, half):
        return ring(p, d, 0, 2, half, far1, 1 if half == 0 else 3)

    def direct(p, d, half):
        side = 3 if half == 0 else 1
        return ring(p, d, 1, side, half, plain1, side)

    def relayed(p, d, half):
        side = 1 if half == 0 else 3
        return ring(p, d, 2, side, half, merged1, side)

    s_second, r_second = sends.take(1), recvs.take(12)
    s_third, r_third = sends.take(1), recvs.take(3)
    s_last, r_last = sends.take(1), recvs.take(1)
    assert sends.count <= SENDS and recvs.count <= RECVS

    def second(p, d, s):
        return wire(
            s_second, r_second + 3 * d + p, z2.at[d, p, s], got2.at[d, p, s - 1],
            place.along(p, 0, s),
        )

    def third(p, d):
        return wire(
            s_third, r_third + p, z3.at[d - 1, p], got3.at[d - 1, p], place.along(p, 2, d)
        )

    last = wire(s_last, r_last, o_ref.at[core], o_ref.at[core], sibling)

    def gate_up(d):
        for n in range(2):
            rows = jnp.concatenate(
                [
                    jnp.concatenate(
                        [x_ref[p, k, d].reshape(QUARTER, width) for k in range(4)], axis=1
                    )
                    for p in range(PARTS)
                ],
                axis=0,
            )
            cols = pl.ds(n * ff, ff)
            result = jnp.dot(rows, w_ref[:, cols], preferred_element_type=F32)
            gate, up = result[:, :block], result[:, block:]
            hidden = gate / (1.0 + jnp.exp(-gate)) * up
            h_ref[:, pl.ds(n * block, block)] = hidden.astype(BF16)

    def down(d):
        def scaled(k):
            scale = jnp.concatenate(
                [weight[p, d].reshape(QUARTER, 128) for p in range(PARTS)], axis=0
            )
            return jnp.dot(h_ref[...], wd_ref[k], preferred_element_type=F32) * jnp.concatenate(
                [scale] * (width // 128), axis=1
            )

        for half in range(2):
            result = scaled(2 * (1 - core) + half).astype(BF16)
            for p in range(PARTS):
                region(p, d, half)[...] = result[p * QUARTER : (p + 1) * QUARTER].reshape(
                    4, GROUP, width
                )
            if d and half == 0:
                pl.semaphore_wait(credit.at[d], 1)
            for p in range(PARTS):
                handed(p, d, half).start()
        for half in range(2):
            result = scaled(2 * core + half)
            arrived(r_hand + 2 * d + half, x_ref.at[0, pl.ds(0, 3), 0])
            for p in range(PARTS):
                ref = region(p, d, 2 + half)
                mine = result[p * QUARTER : (p + 1) * QUARTER].reshape(4, GROUP, width)
                ref[...] = (mine + ref[...].astype(F32)).astype(BF16)
                opposite(p, d, half).start()
                direct(p, d, half).start()

    def free(d):
        pl.semaphore_signal(credit.at[d], inc=1, device_id=sibling, device_id_type=MESH)

    def merge(d):
        @each
        def _(p):
            arrived(r_ring + 3 * d + p, far1.at[d, p])
            for half in range(2):
                ref = region(p, d, 2 + half).at[1 if half == 0 else 3]
                ref[...] = (ref[...].astype(F32) + far1[d, p, half].astype(F32)).astype(BF16)
                relayed(p, d, half).start()

    def total(d):
        @each
        def _(p):
            arrived(r_ring + 12 + 3 * d + p, x_ref.at[0, 0, 0])
            sums = [
                region(p, d, 2 + half)[0].astype(F32)
                + plain1[d, p, half].astype(F32)
                + merged1[d, p, half].astype(F32)
                for half in range(2)
            ]
            for i in range(4):
                rows = [t[i * UNIT : (i + 1) * UNIT] for t in sums]
                z2[d, p, i] = jnp.concatenate(rows, axis=0).astype(BF16)
            for s in (2, 1, 3):
                second(p, d, s).start()

    def chip_sum(p, d):
        arrived(r_second + 3 * d + p, got2.at[d, p])
        result = z2[d, p, 0].astype(F32)
        for s in (1, 2, 3):
            result = result + got2[d, p, s - 1].astype(F32)
        return result

    for s, o in others:
        for p in range(PARTS):
            dealt(p, s, o).start()
    for s, o in others:
        dealt_table(s, o).start()
    for load in loads:
        load.start()
    for p in range(PARTS):
        first[p, core] = t_ref[core, p]
    first_c[core] = c_ref[...]
    for p in range(PARTS):
        arrived(r_deal + p, first.at[p, pl.ds(0, 7)])
        halves = ([], [])
        for i in range(4):
            a, b = first[p, 2 * i].astype(F32), first[p, 2 * i + 1].astype(F32)
            for half in range(2):
                at = half * SHARE
                halves[half].extend([a[at : at + SHARE], b[at : at + SHARE]])
        for half in range(2):
            x_ref[p, 2 * core + half, 0, 0] = jnp.concatenate(halves[half], axis=0).astype(BF16)
        for half, step in ((0, 1), (1, 3), (1, 1), (0, 3)):
            two(p, half, step).start()

    arrived(r_table, first_c.at[pl.ds(0, 7)])
    row8 = lax.broadcasted_iota(jnp.int32, (8, 128), 0)
    table[0, 0] = sum(jnp.where(row8 == i, first_c[i], 0.0) for i in range(8))
    for s in (1, 2, 3):
        table_wire(1, s).start()

    @each
    def _(p):
        for half in range(2):
            arrived(r_two + 3 * half + p, x_ref.at[0, 0, 0, 0])
            two_on(p, half).start()
        three_all(p, False)

    @each
    def _(p):
        arrived(r_two + 6 + p, x_ref.at[0, 0, 0])
        three_all(p, True)
        joined(p, 0).start()

    arrived(r_table + 1, first_c.at[pl.ds(0, 3)])
    for s in (1, 2, 3):
        table_wire(2, s).start()
    for load in loads[:4]:
        load.wait()
    arrived(r_join, half_of_quarter)
    gate_up(0)

    arrived(r_table + 2, table.at[pl.ds(0, 3)])
    lane = lax.broadcasted_iota(jnp.int32, (UNIT, 128), 1)
    row = lax.broadcasted_iota(jnp.int32, (UNIT, 128), 0)
    token = jnp.where(row < SHARE, row, row - SHARE) + place.expert * 16

    @pl.loop(0, 16)
    def _(yz):
        y, z = lax.div(yz, 4), lax.rem(yz, 4)
        rows = table[z, y]
        for x in range(4):
            pair = jnp.where(row < SHARE, rows[2 * x : 2 * x + 1], rows[2 * x + 1 : 2 * x + 2])
            at = (x, y, z)
            for p in range(PARTS):
                chosen = lane == token + p * SHARE
                value = jnp.sum(jnp.where(chosen, pair, 0.0), axis=1, keepdims=True)
                weight[p, at[(p + 2) % 3], at[(p + 1) % 3], at[p]] = jnp.broadcast_to(
                    value, (UNIT, 128)
                )

    for load in loads[4:]:
        load.wait()
    down(0)

    @each
    def _(p):
        for half in range(2):
            arrived(r_three + 3 * half + p, x_ref.at[0, 0, 0])
            for g in range(4):
                three_on(p, half, g).start()
            joined(p, 3 if half == 0 else 1, half).start()

    @each
    def _(p):
        arrived(r_three + 6 + p, x_ref.at[0, pl.ds(0, 2), 0])
        joined(p, 3, 1).start()
        joined(p, 1, 0).start()

    sent(s_two, x_ref.at[:, :, 0, 0])
    sent(s_two + 1, far1.at[0])
    sent(s_three, x_ref.at[:, :, 0])
    sent(s_join, half_of_quarter)
    free(3)
    arrived(r_join + 3, half_of_quarter)
    gate_up(3)
    down(3)

    for g in range(4):
        @each
        def _(p):
            arrived(r_three + 9 + 3 * g + p, x_ref.at[0, 0, 0, pl.ds(0, 2)])
            for half in range(2):
                joined(p, 2, half, g).start()

    sent(s_three + 1, x_ref.at[:, 0, 0])
    sent(s_join + 3, half_of_quarter)
    free(1)
    arrived(r_join + 1, half_of_quarter)
    gate_up(1)
    merge(0)
    sent(s_three + 2, x_ref.at[:, 0, 0])
    sent(s_join + 1, half_of_quarter)
    free(2)
    down(1)
    merge(3)
    arrived(r_join + 2, half_of_quarter)
    gate_up(2)
    total(0)
    merge(1)
    down(2)
    total(3)
    merge(2)
    total(1)

    def finish(d):
        @each
        def _(p):
            z3[d - 1, p] = chip_sum(p, d).astype(BF16)
            third(p, d).start()

    finish(3)
    finish(1)
    total(2)
    finish(2)

    @each
    def _(p):
        result = chip_sum(p, 0)
        arrived(r_third + p, got3.at[:, 0])
        for d in (3, 1, 2):
            result = result + got3[d - 1, p].astype(F32)
        o_ref[core, p] = result.astype(BF16)

    last.start()

    sent(s_deal, first.at[:, pl.ds(0, 7)])
    sent(s_table, first_c.at[pl.ds(0, 7)])
    sent(s_table + 1, first_c.at[pl.ds(0, 3)])
    sent(s_table + 2, table.at[pl.ds(0, 3)])
    sent(s_join + 2, half_of_quarter)
    sent(s_hand, x_ref.at[:, pl.ds(0, 2)])
    sent(s_ring, far1)
    sent(s_ring + 1, far1)
    sent(s_ring + 2, far1)
    sent(s_second, got2)
    sent(s_third, got3)
    last.wait_recv()
    for k in range(4):
        rows = []
        for p in range(PARTS):
            both = o_ref[k // 2, p].astype(F32)
            at = (k % 2) * UNIT
            rows.append(
                jnp.where(core == 0, both[at : at + SHARE], both[at + SHARE : at + 2 * SHARE])
            )
        out_ref[:, k * width : (k + 1) * width] = jnp.concatenate(rows, axis=0).astype(BF16)
    last.wait_send()


def on_device(tokens, routes, combine, gate_weight, up_weight, down_weight):
    model_width = tokens.shape[1]
    width = model_width // 4
    ff = gate_weight.shape[2]
    vmem = pl.BlockSpec(memory_space=pltpu.VMEM)
    hbm = pl.BlockSpec(memory_space=pl.ANY)

    def ring_buffer():
        return pltpu.VMEM((4, PARTS, 2, GROUP, width), BF16)

    return pl.pallas_call(
        kernel,
        out_shape=jax.ShapeDtypeStruct((ROWS, model_width), BF16),
        in_specs=[vmem, vmem, vmem, hbm, hbm, hbm],
        out_specs=vmem,
        scratch_shapes=[
            pltpu.VMEM((model_width, 2 * ff), BF16),
            pltpu.VMEM((4, ff, width), BF16),
            pltpu.VMEM((2, PARTS, 2 * SHARE, width), BF16),
            pltpu.VMEM((8, 128), F32),
            pltpu.VMEM((8, 128), F32),
            pltpu.VMEM((8, 128), jnp.int32),
            pltpu.VMEM((PARTS, 8, 2 * SHARE, width), BF16),
            pltpu.VMEM((8, 8, 128), F32),
            pltpu.VMEM((PARTS, 4, 4, 4, GROUP, width), BF16),
            pltpu.VMEM((PARTS, 4, 4, GROUP, width), BF16),
            pltpu.VMEM((PARTS * QUARTER, ff), BF16),
            pltpu.VMEM((4, 4, 8, 128), F32),
            pltpu.VMEM((PARTS, 4, 4, 4, UNIT, 128), F32),
            ring_buffer(),
            ring_buffer(),
            ring_buffer(),
            pltpu.VMEM((4, PARTS, 4, 2 * UNIT, width), BF16),
            pltpu.VMEM((4, PARTS, 3, 2 * UNIT, width), BF16),
            pltpu.VMEM((3, PARTS, 2 * UNIT, width), BF16),
            pltpu.VMEM((3, PARTS, 2 * UNIT, width), BF16),
            pltpu.VMEM((2, PARTS, 2 * UNIT, width), BF16),
            pltpu.SemaphoreType.DMA((8,)),
            pltpu.SemaphoreType.DMA((SENDS,)),
            pltpu.SemaphoreType.DMA((RECVS,)),
            pltpu.SemaphoreType.REGULAR((4,)),
        ],
        compiler_params=pltpu.CompilerParams(
            collective_id=0, has_side_effects=True, vmem_limit_bytes=62 * 2**20
        ),
    )(tokens, routes.T, combine.T, gate_weight[0], up_weight[0], down_weight[0])


def solution(mesh):
    placed = (
        P(("expert", "hidden"), None),
        P(("expert", "hidden"), None),
        P(("expert", "hidden"), None),
        P("expert", None, "hidden"),
        P("expert", None, "hidden"),
        P("expert", "hidden", None),
    )
    return jax.shard_map(
        on_device,
        mesh=mesh,
        in_specs=placed,
        out_specs=P(("expert", "hidden"), None),
        check_vma=False,
    )
```

```python
import jax
import jax.numpy as jnp
from jax import lax
from jax.experimental import pallas as pl
from jax.experimental.pallas import tpu as pltpu
from jax.sharding import PartitionSpec as P

MESH = pl.DeviceIdType.MESH
BF16, F32 = jnp.bfloat16, jnp.float32
ROWS = 12
PARTS = 3
SHARE = ROWS // PARTS
UNIT = 2 * SHARE
GROUP = 4 * UNIT
QUARTER = 4 * GROUP


def hot(axis):
    if isinstance(axis, int):
        return tuple(int(axis == j) for j in range(3))
    return (lax.div((2 - axis) * (1 - axis), 2), axis * (2 - axis), lax.div(axis * (axis - 1), 2))


class Place:
    def __init__(self):
        e, h = lax.axis_index("expert"), lax.axis_index("hidden")
        self.expert = e
        self.core = lax.rem(e, 2)
        self.at = (
            lax.div(h, 8),
            lax.rem(h, 4),
            lax.rem(lax.div(h, 4), 2) * 2 + lax.div(e, 2),
        )

    def device(self, at, core):
        x, y, z = at
        return {
            "expert": lax.rem(z, 2) * 2 + core,
            "hidden": x * 8 + lax.div(z, 2) * 4 + y,
        }

    def sibling(self):
        return self.device(self.at, 1 - self.core)

    def axis(self, p, k):
        return (p + k) % 3 if isinstance(p, int) else lax.rem(p + k, 3)

    def coord(self, p, k):
        return sum(a * o for a, o in zip(self.at, hot(self.axis(p, k))))

    def along(self, p, k, step, other=0):
        on = hot(self.axis(p, k))
        core = 1 - self.core if other else self.core
        return self.device(tuple(lax.rem(a + step * o, 4) for a, o in zip(self.at, on)), core)

def meet(place):
    barrier = pltpu.get_barrier_semaphore()
    partners = [place.sibling()] + [
        place.along(a, 0, step, other) for a in range(3) for step in (1, 2, 3) for other in (0, 1)
    ]
    for partner in partners:
        pl.semaphore_signal(barrier, inc=1, device_id=partner, device_id_type=MESH)
    pl.semaphore_wait(barrier, len(partners))


def each(body):
    pl.loop(0, PARTS)(body)


def plus(i, n):
    return lax.rem(i + n, 4)


class Slots:
    def __init__(self):
        self.count = 0

    def take(self, n):
        base = self.count
        self.count += n
        return base


SENDS, RECVS = 24, 96


def kernel(
    tok_ref, route_ref, comb_ref, gate_ref, up_ref, down_ref, out_ref,
    w_ref, wd_ref, t_ref, c_ref, pad_c, pad_r, first, first_c, x_ref, y_ref, h_ref, table, weight,
    far1, plain1, merged1, z2, got2, z3, got3,
    load_sem, send_sem, recv_sem, credit,
):
    place = Place()
    core, sibling = place.core, place.sibling()
    width = x_ref.shape[-1]
    ff = gate_ref.shape[1]
    block = ff // 2
    sends, recvs = Slots(), Slots()

    def wire(send, recv, src, dst, device):
        return pltpu.make_async_remote_copy(
            src_ref=src,
            dst_ref=dst,
            send_sem=send_sem.at[send],
            recv_sem=recv_sem.at[recv],
            device_id=device,
            device_id_type=MESH,
        )

    def sent(slot, ref):
        wire(slot, 0, ref, ref, sibling).wait_send()

    def arrived(slot, ref):
        wire(0, slot, ref, ref, sibling).wait_recv()

    loads = []
    for n in range(2):
        for m, ref in enumerate((gate_ref, up_ref)):
            loads.append(
                pltpu.make_async_copy(
                    ref.at[:, pl.ds(n * block, block)],
                    w_ref.at[:, pl.ds((2 * n + m) * block, block)],
                    load_sem.at[len(loads)],
                )
            )
    for k in range(4):
        loads.append(
            pltpu.make_async_copy(
                down_ref.at[:, pl.ds(k * width, width)], wd_ref.at[k], load_sem.at[len(loads)]
            )
        )

    for k in range(4):
        rows = tok_ref[:, k * width : (k + 1) * width].astype(F32)
        for p in range(PARTS):
            at = (k % 2) * SHARE
            t_ref[k // 2, p, at : at + SHARE] = rows[p * SHARE : (p + 1) * SHARE].astype(BF16)
    pad_c[...] = jnp.zeros(pad_c.shape, F32)
    pad_r[...] = jnp.zeros(pad_r.shape, jnp.int32)
    pad_c[0:2, 0:ROWS] = comb_ref[...]
    pad_r[0:2, 0:ROWS] = route_ref[...]
    spread = pad_c[...] * 0.0
    for e in range(4):
        mine = jnp.where(pad_r[...] == e, pad_c[...], 0.0)
        spread = spread + (pltpu.roll(mine, 16 * e, 1) if e else mine)
    c_ref[...] = jnp.broadcast_to(jnp.sum(spread, axis=0, keepdims=True), (8, 128))

    meet(place)

    others = [(s, o) for s in (0, 1, 3, 2) for o in range(2) if (s, o) != (0, 0)]
    s_deal, r_deal = sends.take(1), recvs.take(3)
    s_table, r_table = sends.take(3), recvs.take(3)

    def dealt(p, s, o):
        to = 1 - core if o else core
        return wire(
            s_deal, r_deal + p, t_ref.at[to, p], first.at[p, 2 * ((4 - s) % 4) + core],
            place.along(p, 0, s, o),
        )

    def dealt_table(s, o):
        at = first_c.at[2 * ((4 - s) % 4) + core]
        return wire(s_table, r_table, c_ref, at, place.along(0, 0, s, o))

    def table_wire(k, s):
        if k == 1:
            src, dst = table.at[0, 0], table.at[0, 4 - s]
        else:
            src, dst = table.at[0], table.at[4 - s]
        return wire(s_table + k, r_table + k, src, dst, place.along(0, k, s))

    s_two, r_two = sends.take(2), recvs.take(9)

    def two(p, half, step):
        at = x_ref.at[p, 2 * core + half, 0]
        kind = 0 if half == (0 if step == 1 else 1) else 2
        slot = r_two + (half if kind == 0 else 2) * 3 + p
        return wire(s_two, slot, at.at[0], at.at[4 - step], place.along(p, 1, step))

    def two_on(p, half):
        at = x_ref.at[p, 2 * core + half, 0]
        step = 1 if half == 0 else 3
        return wire(s_two + 1, r_two + 6 + p, at.at[4 - step], at.at[2], place.along(p, 1, step))

    s_three, r_three = sends.take(3), recvs.take(9 + 12)

    def three(p, half, step, rest):
        at = x_ref.at[p, 2 * core + half]
        groups = pl.ds(1, 3) if rest else pl.ds(0, 1)
        kind = half if half == (0 if step == 1 else 1) else 2
        return wire(
            s_three, r_three + kind * 3 + p, at.at[0, groups], at.at[4 - step, groups],
            place.along(p, 2, step),
        )

    def three_all(p, rest):
        for half, step in ((0, 1), (1, 3), (1, 1), (0, 3)):
            three(p, half, step, rest).start()

    def three_on(p, half, g):
        at = x_ref.at[p, 2 * core + half]
        step = 1 if half == 0 else 3
        return wire(
            s_three + 1 + half, r_three + 9 + 3 * g + p, at.at[4 - step, g], at.at[2, g],
            place.along(p, 2, step),
        )

    s_join, r_join = sends.take(4), recvs.take(4)

    def joined(p, d, half=None, g=None):
        if half is None:
            ref = x_ref.at[p, pl.ds(2 * core, 2), d]
        else:
            ref = x_ref.at[p, 2 * core + half, d]
        if g is not None:
            ref = ref.at[g]
        return wire(s_join + d, r_join + d, ref, ref, sibling)

    half_of_quarter = x_ref.at[:, pl.ds(0, 2), 0]

    def region(p, d, k):
        if d == 0:
            return y_ref.at[p, k]
        return x_ref.at[p, k, {3: 0, 1: 3, 2: 1}[d]]

    s_hand, r_hand = sends.take(1), recvs.take(8)

    def handed(p, d, half):
        return wire(
            s_hand, r_hand + 2 * d + half, region(p, d, half), region(p, d, 2 + half), sibling
        )

    s_ring, r_ring = sends.take(3), recvs.take(24)

    def ring(p, d, n, q, half, into, step):
        slot = r_ring + 3 * d + p + (12 if n else 0)
        return wire(
            s_ring + n, slot, region(p, d, 2 + half).at[q], into.at[d, p, half],
            place.along(p, 1, step),
        )

    def opposite(p, d, half):
        return ring(p, d, 0, 2, half, far1, 1 if half == 0 else 3)

    def direct(p, d, half):
        side = 3 if half == 0 else 1
        return ring(p, d, 1, side, half, plain1, side)

    def relayed(p, d, half):
        side = 1 if half == 0 else 3
        return ring(p, d, 2, side, half, merged1, side)

    s_second, r_second = sends.take(1), recvs.take(12)
    s_third, r_third = sends.take(1), recvs.take(3)
    assert sends.count <= SENDS and recvs.count <= RECVS

    def second(p, d, s):
        return wire(
            s_second, r_second + 3 * d + p, z2.at[d, p, s], got2.at[d, p, s - 1],
            place.along(p, 0, s),
        )

    def third(p, d, o):
        to = 1 - core if o else core
        return wire(
            s_third, r_third + p, z3.at[d, p, to], got3.at[o, d, p], place.along(p, 2, d, o)
        )

    def gate_up(d):
        for n in range(2):
            rows = jnp.concatenate(
                [
                    jnp.concatenate(
                        [x_ref[p, k, d].reshape(QUARTER, width) for k in range(4)], axis=1
                    )
                    for p in range(PARTS)
                ],
                axis=0,
            )
            cols = pl.ds(n * ff, ff)
            result = jnp.dot(rows, w_ref[:, cols], preferred_element_type=F32)
            gate, up = result[:, :block], result[:, block:]
            hidden = gate / (1.0 + jnp.exp(-gate)) * up
            h_ref[:, pl.ds(n * block, block)] = hidden.astype(BF16)

    def down(d):
        def scaled(k):
            scale = jnp.concatenate(
                [weight[p, d].reshape(QUARTER, 128) for p in range(PARTS)], axis=0
            )
            return jnp.dot(h_ref[...], wd_ref[k], preferred_element_type=F32) * jnp.concatenate(
                [scale] * (width // 128), axis=1
            )

        for half in range(2):
            result = scaled(2 * (1 - core) + half).astype(BF16)
            for p in range(PARTS):
                region(p, d, half)[...] = result[p * QUARTER : (p + 1) * QUARTER].reshape(
                    4, GROUP, width
                )
            if d and half == 0:
                pl.semaphore_wait(credit.at[d], 1)
            for p in range(PARTS):
                handed(p, d, half).start()
        for half in range(2):
            result = scaled(2 * core + half)
            arrived(r_hand + 2 * d + half, x_ref.at[0, pl.ds(0, 3), 0])
            for p in range(PARTS):
                ref = region(p, d, 2 + half)
                mine = result[p * QUARTER : (p + 1) * QUARTER].reshape(4, GROUP, width)
                ref[...] = (mine + ref[...].astype(F32)).astype(BF16)
                opposite(p, d, half).start()
                direct(p, d, half).start()

    def free(d):
        pl.semaphore_signal(credit.at[d], inc=1, device_id=sibling, device_id_type=MESH)

    def merge(d):
        @each
        def _(p):
            arrived(r_ring + 3 * d + p, far1.at[d, p])
            for half in range(2):
                ref = region(p, d, 2 + half).at[1 if half == 0 else 3]
                ref[...] = (ref[...].astype(F32) + far1[d, p, half].astype(F32)).astype(BF16)
                relayed(p, d, half).start()

    def total(d):
        @each
        def _(p):
            arrived(r_ring + 12 + 3 * d + p, x_ref.at[0, 0, 0])
            sums = [
                region(p, d, 2 + half)[0].astype(F32)
                + plain1[d, p, half].astype(F32)
                + merged1[d, p, half].astype(F32)
                for half in range(2)
            ]
            for i in range(4):
                rows = [t[i * UNIT : (i + 1) * UNIT] for t in sums]
                z2[d, p, i] = jnp.concatenate(rows, axis=0).astype(BF16)
            for s in (2, 1, 3):
                second(p, d, s).start()

    def chip_sum(p, d):
        arrived(r_second + 3 * d + p, got2.at[d, p])
        result = z2[d, p, 0].astype(F32)
        for s in (1, 2, 3):
            result = result + got2[d, p, s - 1].astype(F32)
        return result

    for s, o in others:
        for p in range(PARTS):
            dealt(p, s, o).start()
    for s, o in others:
        dealt_table(s, o).start()
    for load in loads:
        load.start()
    for p in range(PARTS):
        first[p, core] = t_ref[core, p]
    first_c[core] = c_ref[...]
    for p in range(PARTS):
        arrived(r_deal + p, first.at[p, pl.ds(0, 7)])
        halves = ([], [])
        for i in range(4):
            a, b = first[p, 2 * i].astype(F32), first[p, 2 * i + 1].astype(F32)
            for half in range(2):
                at = half * SHARE
                halves[half].extend([a[at : at + SHARE], b[at : at + SHARE]])
        for half in range(2):
            x_ref[p, 2 * core + half, 0, 0] = jnp.concatenate(halves[half], axis=0).astype(BF16)
        for half, step in ((0, 1), (1, 3), (1, 1), (0, 3)):
            two(p, half, step).start()

    arrived(r_table, first_c.at[pl.ds(0, 7)])
    row8 = lax.broadcasted_iota(jnp.int32, (8, 128), 0)
    table[0, 0] = sum(jnp.where(row8 == i, first_c[i], 0.0) for i in range(8))
    for s in (1, 2, 3):
        table_wire(1, s).start()

    @each
    def _(p):
        for half in range(2):
            arrived(r_two + 3 * half + p, x_ref.at[0, 0, 0, 0])
            two_on(p, half).start()
        three_all(p, False)

    @each
    def _(p):
        arrived(r_two + 6 + p, x_ref.at[0, 0, 0])
        three_all(p, True)
        joined(p, 0).start()

    arrived(r_table + 1, first_c.at[pl.ds(0, 3)])
    for s in (1, 2, 3):
        table_wire(2, s).start()
    for load in loads[:4]:
        load.wait()
    arrived(r_join, half_of_quarter)
    gate_up(0)

    arrived(r_table + 2, table.at[pl.ds(0, 3)])
    lane = lax.broadcasted_iota(jnp.int32, (UNIT, 128), 1)
    row = lax.broadcasted_iota(jnp.int32, (UNIT, 128), 0)
    token = jnp.where(row < SHARE, row, row - SHARE) + place.expert * 16

    @pl.loop(0, 16)
    def _(yz):
        y, z = lax.div(yz, 4), lax.rem(yz, 4)
        rows = table[z, y]
        for x in range(4):
            pair = jnp.where(row < SHARE, rows[2 * x : 2 * x + 1], rows[2 * x + 1 : 2 * x + 2])
            at = (x, y, z)
            for p in range(PARTS):
                chosen = lane == token + p * SHARE
                value = jnp.sum(jnp.where(chosen, pair, 0.0), axis=1, keepdims=True)
                weight[p, at[(p + 2) % 3], at[(p + 1) % 3], at[p]] = jnp.broadcast_to(
                    value, (UNIT, 128)
                )

    for load in loads[4:]:
        load.wait()
    down(0)

    @each
    def _(p):
        for half in range(2):
            arrived(r_three + 3 * half + p, x_ref.at[0, 0, 0])
            for g in range(4):
                three_on(p, half, g).start()
            joined(p, 3 if half == 0 else 1, half).start()

    @each
    def _(p):
        arrived(r_three + 6 + p, x_ref.at[0, pl.ds(0, 2), 0])
        joined(p, 3, 1).start()
        joined(p, 1, 0).start()

    sent(s_two, x_ref.at[:, :, 0, 0])
    sent(s_two + 1, far1.at[0])
    sent(s_three, x_ref.at[:, :, 0])
    sent(s_join, half_of_quarter)
    free(3)
    arrived(r_join + 3, half_of_quarter)
    gate_up(3)
    down(3)

    for g in range(4):
        @each
        def _(p):
            arrived(r_three + 9 + 3 * g + p, x_ref.at[0, 0, 0, pl.ds(0, 2)])
            for half in range(2):
                joined(p, 2, half, g).start()

    sent(s_three + 1, x_ref.at[:, 0, 0])
    sent(s_join + 3, half_of_quarter)
    free(1)
    arrived(r_join + 1, half_of_quarter)
    gate_up(1)
    merge(0)
    sent(s_three + 2, x_ref.at[:, 0, 0])
    sent(s_join + 1, half_of_quarter)
    free(2)
    down(1)
    merge(3)
    arrived(r_join + 2, half_of_quarter)
    gate_up(2)
    total(0)
    merge(1)
    down(2)
    total(3)
    merge(2)
    total(1)

    def finish(d):
        @each
        def _(p):
            result = chip_sum(p, d)
            for to in range(2):
                rows = [
                    result[half * UNIT + to * SHARE : half * UNIT + (to + 1) * SHARE]
                    for half in range(2)
                ]
                z3[d, p, to] = jnp.concatenate(rows, axis=0).astype(BF16)
            if d:
                third(p, d, 0).start()
            third(p, d, 1).start()

    finish(0)
    finish(3)
    finish(1)
    total(2)
    finish(2)

    sent(s_deal, first.at[:, pl.ds(0, 7)])
    sent(s_table, first_c.at[pl.ds(0, 7)])
    sent(s_table + 1, first_c.at[pl.ds(0, 3)])
    sent(s_table + 2, table.at[pl.ds(0, 3)])
    sent(s_join + 2, half_of_quarter)
    sent(s_hand, x_ref.at[:, pl.ds(0, 2)])
    sent(s_ring, far1)
    sent(s_ring + 1, far1)
    sent(s_ring + 2, far1)
    sent(s_second, got2)
    columns = ([], [])
    for p in range(PARTS):
        arrived(r_third + p, first.at[p, pl.ds(0, 7)])
        for o in range(2):
            part = z3[0, p, core].astype(F32) if o == 0 else got3[1, 0, p].astype(F32)
            for d in (3, 1, 2):
                part = part + got3[o, d, p].astype(F32)
            columns[o].append(part)
    for half in range(2):
        same, other = [
            jnp.concatenate([c[half * SHARE : (half + 1) * SHARE] for c in columns[o]], axis=0)
            for o in range(2)
        ]
        for k, value in enumerate(
            (jnp.where(core == 0, same, other), jnp.where(core == 0, other, same))
        ):
            at = (2 * k + half) * width
            out_ref[:, at : at + width] = value.astype(BF16)
    sent(s_third, first.at[:, pl.ds(0, 7)])


def on_device(tokens, routes, combine, gate_weight, up_weight, down_weight):
    model_width = tokens.shape[1]
    width = model_width // 4
    ff = gate_weight.shape[2]
    vmem = pl.BlockSpec(memory_space=pltpu.VMEM)
    hbm = pl.BlockSpec(memory_space=pl.ANY)

    def ring_buffer():
        return pltpu.VMEM((4, PARTS, 2, GROUP, width), BF16)

    return pl.pallas_call(
        kernel,
        out_shape=jax.ShapeDtypeStruct((ROWS, model_width), BF16),
        in_specs=[vmem, vmem, vmem, hbm, hbm, hbm],
        out_specs=vmem,
        scratch_shapes=[
            pltpu.VMEM((model_width, 2 * ff), BF16),
            pltpu.VMEM((4, ff, width), BF16),
            pltpu.VMEM((2, PARTS, 2 * SHARE, width), BF16),
            pltpu.VMEM((8, 128), F32),
            pltpu.VMEM((8, 128), F32),
            pltpu.VMEM((8, 128), jnp.int32),
            pltpu.VMEM((PARTS, 8, 2 * SHARE, width), BF16),
            pltpu.VMEM((8, 8, 128), F32),
            pltpu.VMEM((PARTS, 4, 4, 4, GROUP, width), BF16),
            pltpu.VMEM((PARTS, 4, 4, GROUP, width), BF16),
            pltpu.VMEM((PARTS * QUARTER, ff), BF16),
            pltpu.VMEM((4, 4, 8, 128), F32),
            pltpu.VMEM((PARTS, 4, 4, 4, UNIT, 128), F32),
            ring_buffer(),
            ring_buffer(),
            ring_buffer(),
            pltpu.VMEM((4, PARTS, 4, 2 * UNIT, width), BF16),
            pltpu.VMEM((4, PARTS, 3, 2 * UNIT, width), BF16),
            pltpu.VMEM((4, PARTS, 2, 2 * SHARE, width), BF16),
            pltpu.VMEM((2, 4, PARTS, 2 * SHARE, width), BF16),
            pltpu.SemaphoreType.DMA((8,)),
            pltpu.SemaphoreType.DMA((SENDS,)),
            pltpu.SemaphoreType.DMA((RECVS,)),
            pltpu.SemaphoreType.REGULAR((4,)),
        ],
        compiler_params=pltpu.CompilerParams(
            collective_id=0, has_side_effects=True, vmem_limit_bytes=62 * 2**20
        ),
    )(tokens, routes.T, combine.T, gate_weight[0], up_weight[0], down_weight[0])


def solution(mesh):
    placed = (
        P(("expert", "hidden"), None),
        P(("expert", "hidden"), None),
        P(("expert", "hidden"), None),
        P("expert", None, "hidden"),
        P("expert", None, "hidden"),
        P("expert", "hidden", None),
    )
    return jax.shard_map(
        on_device,
        mesh=mesh,
        in_specs=placed,
        out_specs=P(("expert", "hidden"), None),
        check_vma=False,
    )
```

```python
import jax
import jax.numpy as jnp
from jax import lax
from jax.experimental import pallas as pl
from jax.experimental.pallas import tpu as pltpu
from jax.sharding import PartitionSpec as P

MESH = pl.DeviceIdType.MESH
BF16, F32 = jnp.bfloat16, jnp.float32
ROWS = 12
PARTS = 3
SHARE = ROWS // PARTS
UNIT = 2 * SHARE
GROUP = 4 * UNIT
QUARTER = 4 * GROUP


def hot(axis):
    if isinstance(axis, int):
        return tuple(int(axis == j) for j in range(3))
    return (lax.div((2 - axis) * (1 - axis), 2), axis * (2 - axis), lax.div(axis * (axis - 1), 2))


class Place:
    def __init__(self):
        e, h = lax.axis_index("expert"), lax.axis_index("hidden")
        self.expert = e
        self.core = lax.rem(e, 2)
        self.at = (
            lax.div(h, 8),
            lax.rem(h, 4),
            lax.rem(lax.div(h, 4), 2) * 2 + lax.div(e, 2),
        )

    def device(self, at, core):
        x, y, z = at
        return {
            "expert": lax.rem(z, 2) * 2 + core,
            "hidden": x * 8 + lax.div(z, 2) * 4 + y,
        }

    def sibling(self):
        return self.device(self.at, 1 - self.core)

    def axis(self, p, k):
        return (p + k) % 3 if isinstance(p, int) else lax.rem(p + k, 3)

    def coord(self, p, k):
        return sum(a * o for a, o in zip(self.at, hot(self.axis(p, k))))

    def along(self, p, k, step, other=0):
        on = hot(self.axis(p, k))
        core = 1 - self.core if other else self.core
        return self.device(tuple(lax.rem(a + step * o, 4) for a, o in zip(self.at, on)), core)

def meet(place):
    barrier = pltpu.get_barrier_semaphore()
    partners = [place.sibling()] + [
        place.along(a, 0, step, other) for a in range(3) for step in (1, 2, 3) for other in (0, 1)
    ]
    for partner in partners:
        pl.semaphore_signal(barrier, inc=1, device_id=partner, device_id_type=MESH)
    pl.semaphore_wait(barrier, len(partners))


def each(body):
    pl.loop(0, PARTS)(body)


def plus(i, n):
    return lax.rem(i + n, 4)


class Slots:
    def __init__(self):
        self.count = 0

    def take(self, n):
        base = self.count
        self.count += n
        return base


SENDS, RECVS = 24, 96


def kernel(
    tok_ref, route_ref, comb_ref, gate_ref, up_ref, down_ref, out_ref,
    w_ref, wd_ref, t_ref, c_ref, pad_c, pad_r, first, first_c, x_ref, y_ref, h_ref, table, weight,
    far1, plain1, merged1, z2, got2, z3, got3,
    load_sem, send_sem, recv_sem, credit,
):
    place = Place()
    core, sibling = place.core, place.sibling()
    width = x_ref.shape[-1]
    ff = gate_ref.shape[1]
    block = ff // 2
    sends, recvs = Slots(), Slots()

    def wire(send, recv, src, dst, device):
        return pltpu.make_async_remote_copy(
            src_ref=src,
            dst_ref=dst,
            send_sem=send_sem.at[send],
            recv_sem=recv_sem.at[recv],
            device_id=device,
            device_id_type=MESH,
        )

    def sent(slot, ref):
        wire(slot, 0, ref, ref, sibling).wait_send()

    def arrived(slot, ref):
        wire(0, slot, ref, ref, sibling).wait_recv()

    loads = []
    for n in range(2):
        for m, ref in enumerate((gate_ref, up_ref)):
            loads.append(
                pltpu.make_async_copy(
                    ref.at[:, pl.ds(n * block, block)],
                    w_ref.at[:, pl.ds((2 * n + m) * block, block)],
                    load_sem.at[len(loads)],
                )
            )
    for k in range(4):
        loads.append(
            pltpu.make_async_copy(
                down_ref.at[:, pl.ds(k * width, width)], wd_ref.at[k], load_sem.at[len(loads)]
            )
        )

    for k in range(4):
        rows = tok_ref[:, k * width : (k + 1) * width].astype(F32)
        for p in range(PARTS):
            at = (k % 2) * SHARE
            t_ref[k // 2, p, at : at + SHARE] = rows[p * SHARE : (p + 1) * SHARE].astype(BF16)
    pad_c[...] = jnp.zeros(pad_c.shape, F32)
    pad_r[...] = jnp.zeros(pad_r.shape, jnp.int32)
    pad_c[0:2, 0:ROWS] = comb_ref[...]
    pad_r[0:2, 0:ROWS] = route_ref[...]
    spread = pad_c[...] * 0.0
    for e in range(4):
        mine = jnp.where(pad_r[...] == e, pad_c[...], 0.0)
        spread = spread + (pltpu.roll(mine, 16 * e, 1) if e else mine)
    c_ref[...] = jnp.broadcast_to(jnp.sum(spread, axis=0, keepdims=True), (8, 128))

    meet(place)

    others = [(s, o) for s in (0, 1, 3, 2) for o in range(2) if (s, o) != (0, 0)]
    s_deal, r_deal = sends.take(1), recvs.take(3)
    s_table, r_table = sends.take(3), recvs.take(3)

    def dealt(p, s, o):
        to = 1 - core if o else core
        return wire(
            s_deal, r_deal + p, t_ref.at[to, p], first.at[p, 2 * ((4 - s) % 4) + core],
            place.along(p, 0, s, o),
        )

    def dealt_table(s, o):
        at = first_c.at[2 * ((4 - s) % 4) + core]
        return wire(s_table, r_table, c_ref, at, place.along(0, 0, s, o))

    def table_wire(k, s):
        if k == 1:
            src, dst = table.at[0, 0], table.at[0, 4 - s]
        else:
            src, dst = table.at[0], table.at[4 - s]
        return wire(s_table + k, r_table + k, src, dst, place.along(0, k, s))

    s_two, r_two = sends.take(2), recvs.take(9)

    def two(p, half, step):
        at = x_ref.at[p, 2 * core + half, 0]
        kind = 0 if half == (0 if step == 1 else 1) else 2
        slot = r_two + (half if kind == 0 else 2) * 3 + p
        return wire(s_two, slot, at.at[0], at.at[4 - step], place.along(p, 1, step))

    def two_on(p, half):
        at = x_ref.at[p, 2 * core + half, 0]
        step = 1 if half == 0 else 3
        return wire(s_two + 1, r_two + 6 + p, at.at[4 - step], at.at[2], place.along(p, 1, step))

    s_three, r_three = sends.take(3), recvs.take(9 + 12)

    def three(p, half, step, rest):
        at = x_ref.at[p, 2 * core + half]
        groups = pl.ds(1, 3) if rest else pl.ds(0, 1)
        kind = half if half == (0 if step == 1 else 1) else 2
        return wire(
            s_three, r_three + kind * 3 + p, at.at[0, groups], at.at[4 - step, groups],
            place.along(p, 2, step),
        )

    def three_all(p, rest):
        for half, step in ((0, 1), (1, 3), (1, 1), (0, 3)):
            three(p, half, step, rest).start()

    def three_on(p, half, g):
        at = x_ref.at[p, 2 * core + half]
        step = 1 if half == 0 else 3
        return wire(
            s_three + 1 + half, r_three + 9 + 3 * g + p, at.at[4 - step, g], at.at[2, g],
            place.along(p, 2, step),
        )

    s_join, r_join = sends.take(4), recvs.take(4)

    def joined(p, d, half=None, g=None):
        if half is None:
            ref = x_ref.at[p, pl.ds(2 * core, 2), d]
        else:
            ref = x_ref.at[p, 2 * core + half, d]
        if g is not None:
            ref = ref.at[g]
        return wire(s_join + d, r_join + d, ref, ref, sibling)

    half_of_quarter = x_ref.at[:, pl.ds(0, 2), 0]

    def region(p, d, k):
        if d == 0:
            return y_ref.at[p, k]
        return x_ref.at[p, k, {3: 0, 1: 3, 2: 1}[d]]

    s_hand, r_hand = sends.take(1), recvs.take(8)

    def handed(p, d, half):
        return wire(
            s_hand, r_hand + 2 * d + half, region(p, d, half), region(p, d, 2 + half), sibling
        )

    s_ring, r_ring = sends.take(3), recvs.take(24)

    def ring(p, d, n, q, half, into, step):
        slot = r_ring + 3 * d + p + (12 if n else 0)
        return wire(
            s_ring + n, slot, region(p, d, 2 + half).at[q], into.at[d, p, half],
            place.along(p, 1, step),
        )

    def opposite(p, d, half):
        return ring(p, d, 0, 2, half, far1, 1 if half == 0 else 3)

    def direct(p, d, half):
        side = 3 if half == 0 else 1
        return ring(p, d, 1, side, half, plain1, side)

    def relayed(p, d, half):
        side = 1 if half == 0 else 3
        return ring(p, d, 2, side, half, merged1, side)

    s_second, r_second = sends.take(1), recvs.take(12)
    s_third, r_third = sends.take(1), recvs.take(3)
    assert sends.count <= SENDS and recvs.count <= RECVS

    def second(p, d, s):
        return wire(
            s_second, r_second + 3 * d + p, z2.at[d, p, s], got2.at[d, p, s - 1],
            place.along(p, 0, s),
        )

    def third(p, d, o):
        to = 1 - core if o else core
        return wire(
            s_third, r_third + p, z3.at[d, p, to], got3.at[o, d, p], place.along(p, 2, d, o)
        )

    def gate_up(d):
        for n in range(2):
            rows = jnp.concatenate(
                [
                    jnp.concatenate(
                        [x_ref[p, k, d].reshape(QUARTER, width) for k in range(4)], axis=1
                    )
                    for p in range(PARTS)
                ],
                axis=0,
            )
            cols = pl.ds(n * ff, ff)
            result = jnp.dot(rows, w_ref[:, cols], preferred_element_type=F32)
            gate, up = result[:, :block], result[:, block:]
            hidden = gate / (1.0 + jnp.exp(-gate)) * up
            h_ref[:, pl.ds(n * block, block)] = hidden.astype(BF16)

    def down(d):
        def scaled(k):
            scale = jnp.concatenate(
                [weight[p, d].reshape(QUARTER, 128) for p in range(PARTS)], axis=0
            )
            return jnp.dot(h_ref[...], wd_ref[k], preferred_element_type=F32) * jnp.concatenate(
                [scale] * (width // 128), axis=1
            )

        for half in range(2):
            result = scaled(2 * (1 - core) + half).astype(BF16)
            for p in range(PARTS):
                region(p, d, half)[...] = result[p * QUARTER : (p + 1) * QUARTER].reshape(
                    4, GROUP, width
                )
            if d and half == 0:
                pl.semaphore_wait(credit.at[d], 1)
            for p in range(PARTS):
                handed(p, d, half).start()
        for half in range(2):
            result = scaled(2 * core + half)
            arrived(r_hand + 2 * d + half, x_ref.at[0, pl.ds(0, 3), 0])
            for p in range(PARTS):
                ref = region(p, d, 2 + half)
                mine = result[p * QUARTER : (p + 1) * QUARTER].reshape(4, GROUP, width)
                ref[...] = (mine + ref[...].astype(F32)).astype(BF16)
                opposite(p, d, half).start()
                direct(p, d, half).start()

    def free(d):
        pl.semaphore_signal(credit.at[d], inc=1, device_id=sibling, device_id_type=MESH)

    def merge(d):
        @each
        def _(p):
            arrived(r_ring + 3 * d + p, far1.at[d, p])
            for half in range(2):
                ref = region(p, d, 2 + half).at[1 if half == 0 else 3]
                ref[...] = (ref[...].astype(F32) + far1[d, p, half].astype(F32)).astype(BF16)
                relayed(p, d, half).start()

    def total(d):
        @each
        def _(p):
            arrived(r_ring + 12 + 3 * d + p, x_ref.at[0, 0, 0])
            sums = [
                region(p, d, 2 + half)[0].astype(F32)
                + plain1[d, p, half].astype(F32)
                + merged1[d, p, half].astype(F32)
                for half in range(2)
            ]
            for i in range(4):
                rows = [t[i * UNIT : (i + 1) * UNIT] for t in sums]
                z2[d, p, i] = jnp.concatenate(rows, axis=0).astype(BF16)
            for s in (2, 1, 3):
                second(p, d, s).start()

    def chip_sum(p, d):
        arrived(r_second + 3 * d + p, got2.at[d, p])
        result = z2[d, p, 0].astype(F32)
        for s in (1, 2, 3):
            result = result + got2[d, p, s - 1].astype(F32)
        return result

    for s, o in others:
        for p in range(PARTS):
            dealt(p, s, o).start()
    for s, o in others:
        dealt_table(s, o).start()
    for load in loads:
        load.start()
    for p in range(PARTS):
        first[p, core] = t_ref[core, p]
    first_c[core] = c_ref[...]
    for p in range(PARTS):
        arrived(r_deal + p, first.at[p, pl.ds(0, 7)])
        halves = ([], [])
        for i in range(4):
            a, b = first[p, 2 * i].astype(F32), first[p, 2 * i + 1].astype(F32)
            for half in range(2):
                at = half * SHARE
                halves[half].extend([a[at : at + SHARE], b[at : at + SHARE]])
        for half in range(2):
            x_ref[p, 2 * core + half, 0, 0] = jnp.concatenate(halves[half], axis=0).astype(BF16)
        for half, step in ((0, 1), (1, 3), (1, 1), (0, 3)):
            two(p, half, step).start()

    arrived(r_table, first_c.at[pl.ds(0, 7)])
    row8 = lax.broadcasted_iota(jnp.int32, (8, 128), 0)
    table[0, 0] = sum(jnp.where(row8 == i, first_c[i], 0.0) for i in range(8))
    for s in (1, 2, 3):
        table_wire(1, s).start()

    @each
    def _(p):
        for half in range(2):
            arrived(r_two + 3 * half + p, x_ref.at[0, 0, 0, 0])
            two_on(p, half).start()
        three_all(p, False)

    @each
    def _(p):
        arrived(r_two + 6 + p, x_ref.at[0, 0, 0])
        three_all(p, True)
        joined(p, 0).start()

    arrived(r_table + 1, first_c.at[pl.ds(0, 3)])
    for s in (1, 2, 3):
        table_wire(2, s).start()
    for load in loads[:4]:
        load.wait()
    arrived(r_join, half_of_quarter)
    gate_up(0)

    arrived(r_table + 2, table.at[pl.ds(0, 3)])
    lane = lax.broadcasted_iota(jnp.int32, (UNIT, 128), 1)
    row = lax.broadcasted_iota(jnp.int32, (UNIT, 128), 0)
    token = jnp.where(row < SHARE, row, row - SHARE) + place.expert * 16

    @pl.loop(0, 16)
    def _(yz):
        y, z = lax.div(yz, 4), lax.rem(yz, 4)
        rows = table[z, y]
        for x in range(4):
            pair = jnp.where(row < SHARE, rows[2 * x : 2 * x + 1], rows[2 * x + 1 : 2 * x + 2])
            at = (x, y, z)
            for p in range(PARTS):
                chosen = lane == token + p * SHARE
                value = jnp.sum(jnp.where(chosen, pair, 0.0), axis=1, keepdims=True)
                weight[p, at[(p + 2) % 3], at[(p + 1) % 3], at[p]] = jnp.broadcast_to(
                    value, (UNIT, 128)
                )

    for load in loads[4:]:
        load.wait()
    down(0)

    @each
    def _(p):
        for half in range(2):
            arrived(r_three + 3 * half + p, x_ref.at[0, 0, 0])
            for g in range(4):
                three_on(p, half, g).start()
            joined(p, 3 if half == 0 else 1, half).start()

    @each
    def _(p):
        arrived(r_three + 6 + p, x_ref.at[0, pl.ds(0, 2), 0])
        joined(p, 3, 1).start()
        joined(p, 1, 0).start()

    sent(s_two, x_ref.at[:, :, 0, 0])
    sent(s_two + 1, far1.at[0])
    sent(s_three, x_ref.at[:, :, 0])
    sent(s_join, half_of_quarter)
    free(3)
    arrived(r_join + 3, half_of_quarter)
    gate_up(3)
    down(3)

    for g in range(4):
        @each
        def _(p):
            arrived(r_three + 9 + 3 * g + p, x_ref.at[0, 0, 0, pl.ds(0, 2)])
            for half in range(2):
                joined(p, 2, half, g).start()

    sent(s_three + 1, x_ref.at[:, 0, 0])
    sent(s_join + 3, half_of_quarter)
    free(1)
    arrived(r_join + 1, half_of_quarter)
    gate_up(1)
    merge(0)
    sent(s_three + 2, x_ref.at[:, 0, 0])
    sent(s_join + 1, half_of_quarter)
    free(2)
    down(1)
    merge(3)
    arrived(r_join + 2, half_of_quarter)
    gate_up(2)
    merge(1)
    down(2)
    total(0)
    total(3)
    merge(2)
    total(1)

    def finish(d):
        @each
        def _(p):
            result = chip_sum(p, d)
            for to in range(2):
                rows = [
                    result[half * UNIT + to * SHARE : half * UNIT + (to + 1) * SHARE]
                    for half in range(2)
                ]
                z3[d, p, to] = jnp.concatenate(rows, axis=0).astype(BF16)
            if d:
                third(p, d, 0).start()
            third(p, d, 1).start()

    finish(0)
    finish(3)
    finish(1)
    total(2)
    finish(2)

    sent(s_deal, first.at[:, pl.ds(0, 7)])
    sent(s_table, first_c.at[pl.ds(0, 7)])
    sent(s_table + 1, first_c.at[pl.ds(0, 3)])
    sent(s_table + 2, table.at[pl.ds(0, 3)])
    sent(s_join + 2, half_of_quarter)
    sent(s_hand, x_ref.at[:, pl.ds(0, 2)])
    sent(s_ring, far1)
    sent(s_ring + 1, far1)
    sent(s_ring + 2, far1)
    sent(s_second, got2)
    columns = ([], [])
    for p in range(PARTS):
        arrived(r_third + p, first.at[p, pl.ds(0, 7)])
        for o in range(2):
            part = z3[0, p, core].astype(F32) if o == 0 else got3[1, 0, p].astype(F32)
            for d in (3, 1, 2):
                part = part + got3[o, d, p].astype(F32)
            columns[o].append(part)
    for half in range(2):
        same, other = [
            jnp.concatenate([c[half * SHARE : (half + 1) * SHARE] for c in columns[o]], axis=0)
            for o in range(2)
        ]
        for k, value in enumerate(
            (jnp.where(core == 0, same, other), jnp.where(core == 0, other, same))
        ):
            at = (2 * k + half) * width
            out_ref[:, at : at + width] = value.astype(BF16)
    sent(s_third, first.at[:, pl.ds(0, 7)])


def on_device(tokens, routes, combine, gate_weight, up_weight, down_weight):
    model_width = tokens.shape[1]
    width = model_width // 4
    ff = gate_weight.shape[2]
    vmem = pl.BlockSpec(memory_space=pltpu.VMEM)
    hbm = pl.BlockSpec(memory_space=pl.ANY)

    def ring_buffer():
        return pltpu.VMEM((4, PARTS, 2, GROUP, width), BF16)

    return pl.pallas_call(
        kernel,
        out_shape=jax.ShapeDtypeStruct((ROWS, model_width), BF16),
        in_specs=[vmem, vmem, vmem, hbm, hbm, hbm],
        out_specs=vmem,
        scratch_shapes=[
            pltpu.VMEM((model_width, 2 * ff), BF16),
            pltpu.VMEM((4, ff, width), BF16),
            pltpu.VMEM((2, PARTS, 2 * SHARE, width), BF16),
            pltpu.VMEM((8, 128), F32),
            pltpu.VMEM((8, 128), F32),
            pltpu.VMEM((8, 128), jnp.int32),
            pltpu.VMEM((PARTS, 8, 2 * SHARE, width), BF16),
            pltpu.VMEM((8, 8, 128), F32),
            pltpu.VMEM((PARTS, 4, 4, 4, GROUP, width), BF16),
            pltpu.VMEM((PARTS, 4, 4, GROUP, width), BF16),
            pltpu.VMEM((PARTS * QUARTER, ff), BF16),
            pltpu.VMEM((4, 4, 8, 128), F32),
            pltpu.VMEM((PARTS, 4, 4, 4, UNIT, 128), F32),
            ring_buffer(),
            ring_buffer(),
            ring_buffer(),
            pltpu.VMEM((4, PARTS, 4, 2 * UNIT, width), BF16),
            pltpu.VMEM((4, PARTS, 3, 2 * UNIT, width), BF16),
            pltpu.VMEM((4, PARTS, 2, 2 * SHARE, width), BF16),
            pltpu.VMEM((2, 4, PARTS, 2 * SHARE, width), BF16),
            pltpu.SemaphoreType.DMA((8,)),
            pltpu.SemaphoreType.DMA((SENDS,)),
            pltpu.SemaphoreType.DMA((RECVS,)),
            pltpu.SemaphoreType.REGULAR((4,)),
        ],
        compiler_params=pltpu.CompilerParams(
            collective_id=0, has_side_effects=True, vmem_limit_bytes=62 * 2**20
        ),
    )(tokens, routes.T, combine.T, gate_weight[0], up_weight[0], down_weight[0])


def solution(mesh):
    placed = (
        P(("expert", "hidden"), None),
        P(("expert", "hidden"), None),
        P(("expert", "hidden"), None),
        P("expert", None, "hidden"),
        P("expert", None, "hidden"),
        P("expert", "hidden", None),
    )
    return jax.shard_map(
        on_device,
        mesh=mesh,
        in_specs=placed,
        out_specs=P(("expert", "hidden"), None),
        check_vma=False,
    )
```
